512 devices in a mesh: hst: 8 (over z), dev: 64 (over x, y, core).
Axes of the slice: x: 4, y: 8, z: 8, core: 2. Of those that a mesh axis runs over, the one named last changes fastest.
Arguments:
- feats: bfloat16 [131072, 256], P(('hst', 'dev')), may hold values from -6 to 6
- grad_out: bfloat16 [131072, 256], P(('hst', 'dev')), may hold values from -6 to 6
- preact: bfloat16 [131072, 256], P(('hst', 'dev')), may hold values from -6 to 6
- neigh_agg: bfloat16 [131072, 256], P(('hst', 'dev')), may hold values from -6 to 6
- cross_coords: bfloat16 [131072, 64], P(('hst', 'dev')), may hold values from -6 to 6
- w_self: bfloat16 [256, 256], replicated, may hold values from -0.375 to 0.375
- w_neigh: bfloat16 [256, 256], replicated, may hold values from -0.375 to 0.375
- proj: bfloat16 [256, 64], replicated, may hold values from -0.375 to 0.375
- lift: bfloat16 [64, 256], replicated, may hold values from -0.75 to 0.75
- tile_values: bfloat16 [16384, 128, 128], P(('hst', 'dev')), may hold values from -0.21875 to 0.21875
- tile_rows: int32 [512, 32], P(('hst', 'dev')), may hold values from 0 to 1
- tile_cols: int32 [512, 32], P(('hst', 'dev')), may hold values from 0 to 5
- tile_ids: int32 [512, 32], P(('hst', 'dev')), may hold values from 0 to 31
- cross_rows: int32 [512, 8], P(('hst', 'dev')), may hold values from 0 to 1
- cross_cols: int32 [512, 8], P(('hst', 'dev')), may hold values from 0 to 7
- cross_ids: int32 [512, 8], P(('hst', 'dev')), may hold values from 0 to 31
- send_counts: int32 [512, 64], P(('hst', 'dev')), may hold values from 1 to 8, as said below
- recv_rows: int32 [512, 64, 8], P(('hst', 'dev')), may hold values from 0 to 255
- cross_counts: int32 [512, 8], P(('hst', 'dev')), may hold values from 1 to 128, as said below
- cross_recv_rows: int32 [512, 8, 128], P(('hst', 'dev')), may hold values from 0 to 255
Outputs:
- grad_feats: bfloat16 [131072, 256], P(('hst', 'dev'))
- grad_self: float32 [256, 256], replicated
- grad_neigh: float32 [256, 256], replicated
- grad_lift: float32 [64, 256], replicated
- grad_proj: float32 [256, 64], replicated
The draws below stay inside these ranges and needn't reach their ends.
Inputs may be any that keep to these rules, and one draw needn't show every extreme that they name: `send_counts`: slot k toward peer q is live when k < the count; each partition fills all 8 slots toward the next peer of its group. `cross_counts`: slot k toward group g is live when k < the count; each partition fills all 128 slots toward the next group.
All inputs are finite; a program needn't handle non-finite values.
Results may differ from the reference program's by a relative error of at most 0.0058.
Values may be sent and summed in bfloat16 or wider, within the bound.
No kernel may reach another device: no remote copies, remote signals or barrier semaphores. Data moves between devices by JAX's collectives and lax.ppermute only.
A program may use at most 64 MiB of HBM per device.

```python
import math
import jax
import jax.numpy as jnp
from jax import lax

D = 256
RANK = 64
NB = 2
TPB = 16
CAP = 8
XCAP = 128
V = 32
R = 256
PEERS = 64
GROUPS = 8
PARTS_SIZE = 512
NODES = 131072
NT = 32
NC = 8


def draw_send_counts(key, part):
    key = jax.random.fold_in(key, 11)
    base = jax.random.randint(key, (PARTS_SIZE, PEERS), 1, CAP + 1)
    filled = (jnp.arange(PARTS_SIZE)[:, None] + 1) % PEERS == jnp.arange(PEERS)[None, :]
    return jnp.where(filled, CAP, base).astype(jnp.int32)


def draw_cross_counts(key, part):
    key = jax.random.fold_in(key, 23)
    base = jax.random.randint(key, (PARTS_SIZE, GROUPS), 1, XCAP + 1)
    filled = (jnp.arange(PARTS_SIZE)[:, None] // PEERS + 1) % GROUPS == jnp.arange(GROUPS)[None, :]
    return jnp.where(filled, XCAP, base).astype(jnp.int32)


def touch_ends(result, key, smallest, high):
    spot = [jax.random.randint(jax.random.fold_in(key, axis), (), 0, length) for axis, length in enumerate(result.shape)]
    widest = result.shape.index(max(result.shape))
    next_to = spot[:widest] + [(spot[widest] + 1) % result.shape[widest]] + spot[widest + 1:]
    return result.at[tuple(spot)].set(smallest).at[tuple(next_to)].set(high)


def block_scale(rng, dims, split, low, largest):
    loudness = 1.0
    for axis_at, blocks in split:
        steps = jax.random.uniform(jax.random.fold_in(jax.random.fold_in(rng, 6), axis_at), (blocks,), jnp.float32, low / len(split), largest / len(split))
        loudness = loudness * jnp.repeat(jnp.exp(steps), dims[axis_at] // blocks).reshape((-1,) + (1,) * (len(dims) - 1 - axis_at))
    return loudness


def centred(own_key, dims, deviation, most, split=(), dtype=jnp.bfloat16):
    values = deviation * jax.random.normal(own_key, dims, jnp.float32)
    if split:
        values = values * block_scale(own_key, dims, split, -0.22, 0.18)
    return jnp.clip(values, -most, most).astype(dtype)


def setup_inputs(seed: int = 0) -> dict:
    key_of = jax.random.split(jax.random.key(seed), 21)
    feats = centred(key_of[0], (NODES, D), 1.0, 6.0, ((0, 512),))
    grad_out = centred(key_of[1], (NODES, D), 1.0, 6.0, ((0, 512),))
    preact = centred(key_of[2], (NODES, D), 1.0, 6.0, ((0, 512),))
    neigh_agg = centred(key_of[3], (NODES, D), 1.0, 6.0, ((0, 512),))
    cross_coords = centred(key_of[4], (NODES, RANK), 1.0, 6.0, ((0, 512),))
    w_self = centred(key_of[5], (D, D), D ** -0.5, 0.375)
    w_neigh = centred(key_of[6], (D, D), D ** -0.5, 0.375)
    proj = centred(key_of[7], (D, RANK), D ** -0.5, 0.375)
    lift = centred(key_of[8], (RANK, D), RANK ** -0.5, 0.75)
    tile_values = centred(key_of[9], (PARTS_SIZE * V, 128, 128), (128 * (TPB * NB // (NB + PEERS * CAP // 128) + 1)) ** -0.5, 0.21875, ((0, 512),))
    tile_rows = touch_ends(jax.random.randint(key_of[10], (PARTS_SIZE, NT), 0, NB), jax.random.fold_in(key_of[10], 1), 0, NB - 1).astype(jnp.int32)
    tile_cols = touch_ends(jax.random.randint(key_of[11], (PARTS_SIZE, NT), 0, NB + PEERS * CAP // 128), jax.random.fold_in(key_of[11], 1), 0, (NB + PEERS * CAP // 128) - 1).astype(jnp.int32)
    tile_ids = touch_ends(jax.random.randint(key_of[12], (PARTS_SIZE, NT), 0, V), jax.random.fold_in(key_of[12], 1), 0, V - 1).astype(jnp.int32)
    cross_rows = touch_ends(jax.random.randint(key_of[13], (PARTS_SIZE, NC), 0, NB), jax.random.fold_in(key_of[13], 1), 0, NB - 1).astype(jnp.int32)
    cross_cols = touch_ends(jax.random.randint(key_of[14], (PARTS_SIZE, NC), 0, GROUPS * XCAP // 128), jax.random.fold_in(key_of[14], 1), 0, (GROUPS * XCAP // 128) - 1).astype(jnp.int32)
    cross_ids = touch_ends(jax.random.randint(key_of[15], (PARTS_SIZE, NC), 0, V), jax.random.fold_in(key_of[15], 1), 0, V - 1).astype(jnp.int32)
    send_counts = draw_send_counts(jax.random.fold_in(key_of[20], 71), 0)
    recv_rows = touch_ends(jax.random.randint(key_of[17], (PARTS_SIZE, PEERS, CAP), 0, R), jax.random.fold_in(key_of[17], 1), 0, R - 1).astype(jnp.int32)
    cross_counts = draw_cross_counts(jax.random.fold_in(key_of[20], 71), 0)
    cross_recv_rows = touch_ends(jax.random.randint(key_of[19], (PARTS_SIZE, GROUPS, XCAP), 0, R), jax.random.fold_in(key_of[19], 1), 0, R - 1).astype(jnp.int32)
    return dict(feats=feats, grad_out=grad_out, preact=preact, neigh_agg=neigh_agg, cross_coords=cross_coords, w_self=w_self, w_neigh=w_neigh, proj=proj, lift=lift, tile_values=tile_values, tile_rows=tile_rows, tile_cols=tile_cols, tile_ids=tile_ids, cross_rows=cross_rows, cross_cols=cross_cols, cross_ids=cross_ids, send_counts=send_counts, recv_rows=recv_rows, cross_counts=cross_counts, cross_recv_rows=cross_recv_rows)


def tile_product(tile_vals, row_blocks, col_blocks, tile_index, grads, blocks):
    features = grads.shape[1]
    pieces = grads.reshape(-1, 128, features)[row_blocks].astype(jnp.float32)
    chosen = tile_vals[tile_index].astype(jnp.float32)
    product = jnp.einsum('tij,tif->tjf', chosen, pieces)
    summed = jax.ops.segment_sum(product, col_blocks, num_segments=blocks)
    return summed.reshape(blocks * 128, features)

def land_rows(target_rows, arrived, features):
    start = jnp.zeros((R, features), jnp.float32)
    return start.at[target_rows].add(arrived.astype(jnp.float32))

def reference(feats, grad_out, preact, neigh_agg, cross_coords, w_self, w_neigh, proj, lift, tile_values, tile_rows, tile_cols, tile_ids, cross_rows, cross_cols, cross_ids, send_counts, recv_rows, cross_counts, cross_recv_rows):
    norm_scale = 1.0 / math.sqrt(NODES)
    grad_pre = jnp.where(preact > 0, grad_out.astype(jnp.float32), 0.0).astype(jnp.bfloat16)
    grad_self = norm_scale * jnp.dot(feats.T, grad_pre, preferred_element_type=jnp.float32)
    grad_neigh = norm_scale * jnp.dot(neigh_agg.T, grad_pre, preferred_element_type=jnp.float32)
    grad_lift = norm_scale * jnp.dot(cross_coords.T, grad_pre, preferred_element_type=jnp.float32)
    neigh_grad = jnp.dot(grad_pre, w_neigh.T, preferred_element_type=jnp.float32).astype(jnp.bfloat16)
    coord_grad = jnp.dot(grad_pre, lift.T, preferred_element_type=jnp.float32).astype(jnp.bfloat16)
    col_total = NB + PEERS * CAP // 128
    cross_total = GROUPS * XCAP // 128
    values_all = tile_values.reshape(PARTS_SIZE, V, 128, 128)
    slot_index = jnp.arange(CAP)
    cross_slot = jnp.arange(XCAP)

    def one_part(entry):
        tile_vals, trow, tcol, tidx, xrow, xcol, xidx, neigh_part, coord_part, counts_in, xcounts_in = entry
        inner_sum = tile_product(tile_vals, trow, tcol, tidx, neigh_part, col_total)
        boundary = inner_sum[R:].reshape(PEERS, CAP, D)
        live_mask = slot_index[None, :] < counts_in[:, None]
        boundary = jnp.where(live_mask[:, :, None], boundary, 0.0).astype(jnp.bfloat16)
        cross_sum = tile_product(tile_vals, xrow, xcol, xidx, coord_part, cross_total).reshape(GROUPS, XCAP, RANK)
        cross_mask = cross_slot[None, :] < xcounts_in[:, None]
        cross_part = jnp.where(cross_mask[:, :, None], cross_sum, 0.0).astype(jnp.bfloat16)
        return (inner_sum[:R], boundary, cross_part)
    local_part, boundary, cross_part = lax.map(one_part, (values_all, tile_rows, tile_cols, tile_ids, cross_rows, cross_cols, cross_ids, neigh_grad.reshape(PARTS_SIZE, R, D), coord_grad.reshape(PARTS_SIZE, R, RANK), send_counts, cross_counts))
    boundary_in = jnp.swapaxes(boundary.reshape(GROUPS, PEERS, PEERS, CAP, D), 1, 2).reshape(PARTS_SIZE, PEERS * CAP, D)
    cross_in = jnp.transpose(cross_part.reshape(GROUPS, PEERS, GROUPS, XCAP, RANK), (2, 1, 0, 3, 4)).reshape(PARTS_SIZE, GROUPS * XCAP, RANK)
    landed = jax.vmap(lambda rows_in, arrived: land_rows(rows_in, arrived, D))(recv_rows.reshape(PARTS_SIZE, PEERS * CAP), boundary_in)
    coords = jax.vmap(lambda rows_in, arrived: land_rows(rows_in, arrived, RANK))(cross_recv_rows.reshape(PARTS_SIZE, GROUPS * XCAP), cross_in)
    coords = coords.astype(jnp.bfloat16).reshape(NODES, RANK)
    grad_proj = norm_scale * jnp.dot(feats.T, coords, preferred_element_type=jnp.float32)
    grad_feats = jnp.dot(grad_pre, w_self.T, preferred_element_type=jnp.float32)
    grad_feats = grad_feats + local_part.reshape(NODES, D) + landed.reshape(NODES, D)
    grad_feats = grad_feats + jnp.dot(coords, proj.T, preferred_element_type=jnp.float32)
    return (grad_feats.astype(jnp.bfloat16), grad_self, grad_neigh, grad_lift, grad_proj)
```

```python
import math

import jax
import jax.numpy as jnp
from jax import lax
from jax.experimental import pallas as pl
from jax.experimental.pallas import tpu as pltpu
from jax.sharding import PartitionSpec as P

F32 = jnp.float32
BF16 = jnp.bfloat16
BLOCK = 128

VMEM = pl.BlockSpec(memory_space=pltpu.VMEM)
SMEM = pl.BlockSpec(memory_space=pltpu.SMEM)


def dot_nn(a, b):
    return jnp.dot(a, b, preferred_element_type=F32)


def dot_nt(a, b):
    return lax.dot_general(a, b, (((1,), (1,)), ((), ())), preferred_element_type=F32)


def dot_tn(a, b):
    return lax.dot_general(a, b, (((0,), (0,)), ((), ())), preferred_element_type=F32)


def call(kernel, outs, specs, args, scratch=(), flops=0):
    nbytes = sum(math.prod(o.shape) * o.dtype.itemsize for o in list(outs) + list(args))
    return pl.pallas_call(
        kernel,
        out_shape=tuple(outs),
        in_specs=specs,
        out_specs=tuple(VMEM for _ in outs),
        scratch_shapes=list(scratch),
        compiler_params=pltpu.CompilerParams(vmem_limit_bytes=40 * 1024 * 1024),
        cost_estimate=pl.CostEstimate(flops=flops, bytes_accessed=nbytes, transcendentals=0),
    )(*args)


def shape(dims, dtype):
    return jax.ShapeDtypeStruct(dims, dtype)


def first_kernel(
    xrow, xcol, xid, xcount, grad_out, preact, feats, neigh_agg, cross_coords, lift, tiles,
    gp_out, s1_out, lift_out, cg, acc,
):
    groups = acc.shape[0]
    rank = acc.shape[1]
    gp = jnp.where(preact[...].astype(F32) > 0, grad_out[...].astype(F32), 0.0).astype(BF16)
    gp_out[...] = gp
    cgt = dot_nt(lift[...], gp).astype(BF16)
    for b in range(cg.shape[0]):
        cg[b] = cgt[:, b * BLOCK : (b + 1) * BLOCK]
    acc[...] = jnp.zeros_like(acc)
    for t in range(xrow.shape[1]):
        col = xcol[0, t]
        acc[col] += dot_nn(cg[xrow[0, t]], tiles[xid[0, t]])
    slot = lax.broadcasted_iota(jnp.int32, (rank, BLOCK), 1)
    for j in range(groups):
        s1_out[j, 0:rank, :] = jnp.where(slot < xcount[0, j], acc[j], 0.0).astype(BF16)
    at = rank
    for source in (feats, neigh_agg):
        part = dot_tn(source[...], gp).astype(BF16)
        step = part.shape[0] // groups
        for j in range(groups):
            rows = part[j * step : (j + 1) * step]
            s1_out[j, at : at + step, :] = rows[:, :BLOCK]
            s1_out[j, at + step : at + 2 * step, :] = rows[:, BLOCK:]
        at += 2 * step
    lift_out[...] = dot_tn(cross_coords[...], gp)


def inner_kernel(trow, tcol, tid, counts, gp, w_neigh, w_self, tiles, base_out, bnd_out, ng, acc):
    cap = bnd_out.shape[1]
    blocks = ng.shape[0]
    own = dot_nt(gp[...], w_self[...])
    grad = dot_nt(gp[...], w_neigh[...]).astype(BF16)
    for b in range(blocks):
        ng[b] = grad[b * BLOCK : (b + 1) * BLOCK]
    acc[...] = jnp.zeros_like(acc)
    for t in range(trow.shape[1]):
        col = tcol[0, t]
        acc[col] += dot_tn(tiles[tid[0, t]], ng[trow[0, t]])
    for b in range(blocks):
        base_out[b * BLOCK : (b + 1) * BLOCK, :] = own[b * BLOCK : (b + 1) * BLOCK] + acc[b]
    slot = lax.broadcasted_iota(jnp.int32, (cap, acc.shape[2]), 0)
    per_block = BLOCK // cap
    for q in range(bnd_out.shape[0]):
        rows = acc[blocks + q // per_block, (q % per_block) * cap : (q % per_block + 1) * cap, :]
        bnd_out[q] = jnp.where(slot < counts[0, q], rows, 0.0)


def split_rows(value):
    high = value.astype(BF16).astype(F32)
    return high, value - high


def second_kernel(s1, xrecv, feats, lift_part, bnd, coords_out, s2_out, scr):
    groups = s1.shape[0]
    rank = lift_part.shape[0]
    peers = bnd.shape[0]
    cap = bnd.shape[1]
    nodes = feats.shape[0]
    row = lax.broadcasted_iota(jnp.int32, (nodes, BLOCK), 0)
    total = None
    for g in range(groups):
        hot = jnp.where(row == xrecv[g : g + 1, :], 1.0, 0.0).astype(BF16)
        term = dot_nt(s1[g, 0:rank, :], hot)
        total = term if total is None else total + term
    coords_t = total.astype(BF16)
    coords_out[...] = total.T.astype(BF16)
    proj_t = dot_nn(coords_t, feats[...])
    summed = s1[0, rank:, :].astype(F32)
    for g in range(1, groups):
        summed = summed + s1[g, rank:, :].astype(F32)
    scr[...] = jnp.zeros_like(scr)
    wide = 2 * cap
    for q in range(peers):
        scr[0, q * wide : q * wide + cap, :] = bnd[q, :, :BLOCK]
        scr[1, q * wide : q * wide + cap, :] = bnd[q, :, BLOCK:]
    for half in range(2):
        lanes = slice(half * BLOCK, (half + 1) * BLOCK)
        pieces = (
            summed[half * peers : (half + 1) * peers],
            proj_t[:, lanes],
            lift_part[:, lanes],
        )
        for at, piece in enumerate(pieces):
            high, low = split_rows(piece)
            scr[half, pl.ds(cap + at, peers, stride=wide), :] = high
            scr[half, pl.ds(cap + 3 + at, peers, stride=wide), :] = low
        s2_out[:, lanes] = scr[half].astype(BF16)


def third_kernel(s2, s3_out):
    count = s2.shape[0]
    wide = 16
    kind = lax.rem(lax.broadcasted_iota(jnp.int32, (16, count), 1), wide) - wide // 2
    want = lax.broadcasted_iota(jnp.int32, (16, count), 0)
    pick = (want < 3) & ((kind == want) | (kind == want + 3))
    sums = dot_nn(jnp.where(pick, 1.0, 0.0).astype(BF16), s2[...])
    flat = jnp.concatenate(
        [sums[i : i + 1, h * BLOCK : (h + 1) * BLOCK] for i in range(3) for h in range(2)]
        + [jnp.zeros((2, BLOCK), F32)],
        axis=0,
    )
    for j in range(s3_out.shape[0]):
        s3_out[j] = flat


def feats_kernel(s2, recv, base, coords, proj, out):
    nodes = base.shape[0]
    row = lax.broadcasted_iota(jnp.int32, (nodes, recv.shape[1]), 0)
    hot = jnp.where(row == recv[...], 1.0, 0.0).astype(BF16)
    value = base[...] + dot_nn(hot, s2[...]) + dot_nt(coords[...], proj[...])
    out[...] = value.astype(BF16)


def fourth_kernel(s3, s4_out):
    groups = s3.shape[0]
    total = s3[0]
    for g in range(1, groups):
        total = total + s3[g]
    share = jnp.concatenate(
        [s3[g, 0:1, :] for g in range(groups)]
        + [s3[g, 1:2, :] for g in range(groups)]
        + [total[2:6], jnp.zeros((4, BLOCK), F32)],
        axis=0,
    ).astype(BF16)
    for j in range(s4_out.shape[0]):
        s4_out[j] = share


def last_kernel(norm_scale, s4, self_out, neigh_out, lift_out, proj_out, scr):
    peers, rows = s4.shape[0], s4.shape[1]
    half = peers // 2
    for j in range(peers):
        scr[j * rows : (j + 1) * rows, :] = s4[j].astype(F32) * norm_scale
    for at, out in ((0, self_out), (8, neigh_out)):
        for g in range(8):
            for h in range(2):
                out[g * half : (g + 1) * half, h * BLOCK : (h + 1) * BLOCK] = scr[
                    pl.ds(h * half * rows + at + g, half, stride=rows), :
                ]
    for h in range(2):
        piece = scr[pl.ds(16 + h, peers, stride=rows), :]
        proj_out[h * BLOCK : (h + 1) * BLOCK, :] = piece.T
        lift_out[:, h * BLOCK : (h + 1) * BLOCK] = scr[pl.ds(18 + h, peers, stride=rows), :]


def body(
    feats,
    grad_out,
    preact,
    neigh_agg,
    cross_coords,
    w_self,
    w_neigh,
    proj,
    lift,
    tile_values,
    tile_rows,
    tile_cols,
    tile_ids,
    cross_rows,
    cross_cols,
    cross_ids,
    send_counts,
    recv_rows,
    cross_counts,
    cross_recv_rows,
):
    nodes, width = feats.shape
    rank = proj.shape[1]
    peers = lax.axis_size("dev")
    groups = lax.axis_size("hst")
    cap = recv_rows.shape[-1]
    blocks = nodes // BLOCK
    norm_scale = 1.0 / math.sqrt(nodes * peers * groups)
    wide = 2 * cap

    gp, s1, lift_part = call(
        first_kernel,
        (
            shape((nodes, width), BF16),
            shape((groups, rank + 4 * width // groups, BLOCK), BF16),
            shape((rank, width), F32),
        ),
        [SMEM] * 4 + [VMEM] * 7,
        (cross_rows, cross_cols, cross_ids, cross_counts, grad_out, preact, feats, neigh_agg,
         cross_coords, lift, tile_values),
        [pltpu.VMEM((blocks, rank, BLOCK), BF16), pltpu.VMEM((groups, rank, BLOCK), F32)],
        flops=100_000_000,
    )
    s1 = lax.all_to_all(s1, "hst", split_axis=0, concat_axis=0, tiled=True)
    columns = blocks + peers * cap // BLOCK
    base, bnd = call(
        inner_kernel,
        (shape((nodes, width), F32), shape((peers, cap, width), F32)),
        [SMEM] * 4 + [VMEM] * 4,
        (tile_rows, tile_cols, tile_ids, send_counts, gp, w_neigh, w_self, tile_values),
        [pltpu.VMEM((blocks, BLOCK, width), BF16), pltpu.VMEM((columns, BLOCK, width), F32)],
        flops=350_000_000,
    )
    coords, s2 = call(
        second_kernel,
        (shape((nodes, rank), BF16), shape((peers * wide, width), BF16)),
        [VMEM] * 5,
        (s1, cross_recv_rows.reshape(groups, BLOCK), feats, lift_part, bnd),
        [pltpu.VMEM((2, peers * wide, BLOCK), F32)],
        flops=50_000_000,
    )
    s2 = lax.all_to_all(
        s2.reshape(peers, wide, width), "dev", split_axis=0, concat_axis=0, tiled=True
    ).reshape(peers * wide, width)
    recv = jnp.concatenate(
        [recv_rows.reshape(peers, cap), jnp.full((peers, cap), -1, jnp.int32)], axis=1
    ).reshape(1, peers * wide)
    (s3,) = call(third_kernel, (shape((groups, 8, BLOCK), F32),), [VMEM], (s2,), flops=10_000_000)
    s3 = lax.all_to_all(s3, "hst", split_axis=0, concat_axis=0, tiled=True)
    (grad_feats,) = call(
        feats_kernel,
        (shape((nodes, width), BF16),),
        [VMEM] * 5,
        (s2, recv, base, coords, proj),
        flops=150_000_000,
    )
    (s4,) = call(fourth_kernel, (shape((peers, 24, BLOCK), BF16),), [VMEM], (s3,))
    s4 = lax.all_to_all(s4, "dev", split_axis=0, concat_axis=0, tiled=True)
    grad_self, grad_neigh, grad_lift, grad_proj = call(
        lambda *refs: last_kernel(norm_scale, *refs),
        (
            shape((width, width), F32),
            shape((width, width), F32),
            shape((rank, width), F32),
            shape((width, rank), F32),
        ),
        [VMEM],
        (s4,),
        [pltpu.VMEM((peers * 24, BLOCK), F32)],
    )
    return (grad_feats, grad_self, grad_neigh, grad_lift, grad_proj)


def solution(mesh):
    both = ("hst", "dev")
    row, cube = P(both, None), P(both, None, None)
    placed = (
        (row,) * 5 + (P(),) * 4 + (cube,) + (row,) * 7 + (cube,) + (row,) + (cube,)
    )
    return jax.shard_map(
        body,
        mesh=mesh,
        in_specs=placed,
        out_specs=(row, P(), P(), P(), P()),
        check_vma=False,
    )
```

```python
import math

import jax
import jax.numpy as jnp
from jax import lax
from jax.experimental import pallas as pl
from jax.experimental.pallas import tpu as pltpu
from jax.sharding import PartitionSpec as P

F32 = jnp.float32
BF16 = jnp.bfloat16
BLOCK = 128

VMEM = pl.BlockSpec(memory_space=pltpu.VMEM)
SMEM = pl.BlockSpec(memory_space=pltpu.SMEM)
HBM = pl.BlockSpec(memory_space=pltpu.HBM)


def dot_nn(a, b):
    return jnp.dot(a, b, preferred_element_type=F32)


def dot_nt(a, b):
    return lax.dot_general(a, b, (((1,), (1,)), ((), ())), preferred_element_type=F32)


def dot_tn(a, b):
    return lax.dot_general(a, b, (((0,), (0,)), ((), ())), preferred_element_type=F32)


def call(kernel, outs, specs, args, scratch=(), flops=0, limit=40):
    nbytes = sum(math.prod(o.shape) * o.dtype.itemsize for o in list(outs) + list(args))
    return pl.pallas_call(
        kernel,
        out_shape=tuple(outs),
        in_specs=specs,
        out_specs=tuple(VMEM for _ in outs),
        scratch_shapes=list(scratch),
        compiler_params=pltpu.CompilerParams(vmem_limit_bytes=limit * 1024 * 1024),
        cost_estimate=pl.CostEstimate(flops=flops, bytes_accessed=nbytes, transcendentals=0),
    )(*args)


def shape(dims, dtype):
    return jax.ShapeDtypeStruct(dims, dtype)


def first_kernel(
    xrow_in, xcol_in, xid_in, xcount_in, grad_in, preact_in, lift_in, tiles_in, feats_in, agg_in, coords_in,
    gp_out, s1_out, lift_out,
    xrow, xcol, xid, xcount, grad, preact, lift, tiles, feats, agg, cross, cg, acc, sems,
):
    groups = acc.shape[0]
    rank = acc.shape[1]
    pairs = (
        (grad_in, grad), (preact_in, preact), (lift_in, lift), (xrow_in, xrow), (xcol_in, xcol),
        (xid_in, xid), (xcount_in, xcount), (tiles_in, tiles), (feats_in, feats), (agg_in, agg),
        (coords_in, cross),
    )
    copies = [
        pltpu.make_async_copy(source, target, sems.at[i])
        for i, (source, target) in enumerate(pairs)
    ]
    for copy in copies:
        copy.start()
    for copy in copies[:3]:
        copy.wait()
    gp = jnp.where(preact[...].astype(F32) > 0, grad[...].astype(F32), 0.0).astype(BF16)
    gp_out[...] = gp
    cgt = dot_nt(lift[...], gp).astype(BF16)
    for b in range(cg.shape[0]):
        cg[b] = cgt[:, b * BLOCK : (b + 1) * BLOCK]
    acc[...] = jnp.zeros_like(acc)
    for copy in copies[3:8]:
        copy.wait()
    for t in range(xrow.shape[1]):
        col = xcol[0, t]
        acc[col] += dot_nn(cg[xrow[0, t]], tiles[xid[0, t]])
    slot = lax.broadcasted_iota(jnp.int32, (rank, BLOCK), 1)
    for j in range(groups):
        s1_out[j, 0:rank, :] = jnp.where(slot < xcount[0, j], acc[j], 0.0).astype(BF16)
    at = rank
    for copy, source in ((copies[8], feats), (copies[9], agg)):
        copy.wait()
        part = dot_tn(source[...], gp).astype(BF16)
        step = part.shape[0] // groups
        for j in range(groups):
            rows = part[j * step : (j + 1) * step]
            s1_out[j, at : at + step, :] = rows[:, :BLOCK]
            s1_out[j, at + step : at + 2 * step, :] = rows[:, BLOCK:]
        at += 2 * step
    copies[10].wait()
    lift_out[...] = dot_nn(cross[...], gp)


def inner_kernel(trow, tcol, tid, counts, gp, w_neigh, w_self, tiles, base_out, bnd_out, ng, acc):
    cap = bnd_out.shape[1]
    blocks = ng.shape[0]
    own = dot_nt(gp[...], w_self[...])
    grad = dot_nt(gp[...], w_neigh[...]).astype(BF16)
    for b in range(blocks):
        ng[b] = grad[b * BLOCK : (b + 1) * BLOCK]
    acc[...] = jnp.zeros_like(acc)
    for t in range(trow.shape[1]):
        col = tcol[0, t]
        acc[col] += dot_tn(tiles[tid[0, t]], ng[trow[0, t]])
    for b in range(blocks):
        base_out[b * BLOCK : (b + 1) * BLOCK, :] = own[b * BLOCK : (b + 1) * BLOCK] + acc[b]
    slot = lax.broadcasted_iota(jnp.int32, (cap, acc.shape[2]), 0)
    per_block = BLOCK // cap
    for q in range(bnd_out.shape[0]):
        rows = acc[blocks + q // per_block, (q % per_block) * cap : (q % per_block + 1) * cap, :]
        bnd_out[q] = jnp.where(slot < counts[0, q], rows, 0.0)


def second_kernel(s1, xrecv, feats, lift_part, bnd, coords_out, s2_out, scr):
    groups = s1.shape[0]
    rank = lift_part.shape[0]
    peers = bnd.shape[0]
    cap = bnd.shape[1]
    nodes = feats.shape[0]
    wide = 3 * cap
    row = lax.broadcasted_iota(jnp.int32, (nodes, BLOCK), 0)
    total = None
    for g in range(groups):
        hot = jnp.where(row == xrecv[g : g + 1, :], 1.0, 0.0).astype(BF16)
        term = dot_nt(s1[g, 0:rank, :], hot)
        total = term if total is None else total + term
    coords_t = total.astype(BF16)
    coords_out[...] = total.T.astype(BF16)
    proj_t = dot_nn(coords_t, feats[...])
    summed = s1[0, rank:, :].astype(F32)
    for g in range(1, groups):
        summed = summed + s1[g, rank:, :].astype(F32)
    for q in range(peers):
        scr[q * wide : q * wide + cap, :] = bnd[q, :, :BLOCK]
        scr[q * wide + cap : q * wide + 2 * cap, :] = bnd[q, :, BLOCK:]
    low = proj_t - proj_t.astype(BF16).astype(F32)
    pieces = [summed[:peers], summed[peers:]]
    for value in (proj_t, lift_part[...], low):
        pieces += [value[:, :BLOCK], value[:, BLOCK:]]
    for at, piece in enumerate(pieces):
        scr[pl.ds(2 * cap + at, peers, stride=wide), :] = piece
    s2_out[...] = scr[...].astype(BF16)


def third_kernel(s2, s3_out):
    parts = [s2[q, 16:24, :].astype(F32) for q in range(s2.shape[0])]
    while len(parts) > 1:
        parts = [parts[i] + parts[i + 1] for i in range(0, len(parts), 2)]
    sums = parts[0]
    proj = sums[2:4] + sums[6:8]
    low = proj - proj.astype(BF16).astype(F32)
    share = jnp.concatenate([sums[0:2], proj, sums[4:6], low], axis=0).astype(BF16)
    for j in range(s3_out.shape[0]):
        s3_out[j] = share


def feats_kernel(s2, recv, base, coords, proj_t, out):
    nodes = base.shape[0]
    row = lax.broadcasted_iota(jnp.int32, (nodes, recv.shape[1]), 0)
    for half in range(2):
        lanes = slice(half * BLOCK, (half + 1) * BLOCK)
        hot = jnp.where(row == recv[half : half + 1, :], 1.0, 0.0).astype(BF16)
        value = base[:, lanes] + dot_nn(hot, s2[...]) + dot_nn(coords[...], proj_t[:, lanes])
        out[:, lanes] = value.astype(BF16)


def fourth_kernel(s3, s4_out, scr):
    for j in range(s3.shape[0]):
        scr[j * 8 : (j + 1) * 8, :] = s3[j].astype(F32)
    peers = s3.shape[0]
    side = peers // 8
    pieces = [scr[pl.ds(at, peers, stride=8), :] for at in range(2)]

    def over_groups(at):
        total = scr[pl.ds(at, side, stride=8), :]
        for g in range(1, 8):
            total = total + scr[pl.ds(g * side * 8 + at, side, stride=8), :]
        return total

    for at in range(2):
        pieces.append(over_groups(2 + at) + over_groups(6 + at))
    for at in range(2):
        pieces.append(over_groups(4 + at))
    share = jnp.concatenate(pieces, axis=0).astype(BF16)
    for j in range(s4_out.shape[0]):
        s4_out[j] = share


def last_kernel(norm_scale, s4, self_out, neigh_out, lift_out, proj_out, square, flat):
    groups = 8
    for j in range(s4.shape[0]):
        value = s4[j].astype(F32) * norm_scale
        first = 16 * (j // 2) + j % 2
        for kind in range(2):
            for g in range(groups):
                at = 64 * kind + 8 * g
                square[2 * kind + first // 32, pl.ds(32 * g + first % 32, 8, stride=2), :] = value[
                    at : at + 8
                ]
        for part in range(4):
            at = 128 + 8 * part
            flat[part, pl.ds(first, 8, stride=2), :] = value[at : at + 8]
    for h in range(2):
        lanes = slice(h * BLOCK, (h + 1) * BLOCK)
        self_out[:, lanes] = square[h]
        neigh_out[:, lanes] = square[2 + h]
        proj_out[:, lanes] = flat[h]
        lift_out[:, lanes] = flat[2 + h]


def device_groups(inner):
    sizes = (("z", 8), ("x", 4), ("y", 8), ("core", 2))
    lists = {}
    for z in range(8):
        for x in range(4):
            for y in range(8):
                for core in range(2):
                    place = {"z": z, "x": x, "y": y, "core": core}
                    key = tuple(place[name] for name, _ in sizes if name not in inner)
                    lists.setdefault(key, []).append(((z * 4 + x) * 8 + y) * 2 + core)
    return [lists[key] for key in sorted(lists)]


def body(
    feats,
    grad_out,
    preact,
    neigh_agg,
    cross_coords,
    w_self,
    w_neigh,
    proj,
    lift,
    tile_values,
    tile_rows,
    tile_cols,
    tile_ids,
    cross_rows,
    cross_cols,
    cross_ids,
    send_counts,
    recv_rows,
    cross_counts,
    cross_recv_rows,
):
    nodes, width = feats.shape
    rank = proj.shape[1]
    peers = lax.axis_size("dev")
    groups = lax.axis_size("hst")
    cap = recv_rows.shape[-1]
    blocks = nodes // BLOCK
    norm_scale = 1.0 / math.sqrt(nodes * peers * groups)
    wide = 3 * cap
    both = ("hst", "dev")

    first_args = (
        cross_rows, cross_cols, cross_ids, cross_counts, grad_out, preact, lift, tile_values,
        feats, neigh_agg, cross_coords.T,
    )
    gp, s1, lift_part = call(
        first_kernel,
        (
            shape((nodes, width), BF16),
            shape((groups, rank + 4 * width // groups, BLOCK), BF16),
            shape((rank, width), F32),
        ),
        [HBM] * 11,
        first_args,
        [pltpu.SMEM(v.shape, v.dtype) for v in first_args[:4]]
        + [pltpu.VMEM(v.shape, v.dtype) for v in first_args[4:]]
        + [
            pltpu.VMEM((blocks, rank, BLOCK), BF16),
            pltpu.VMEM((groups, rank, BLOCK), F32),
            pltpu.SemaphoreType.DMA((11,)),
        ],
        flops=100_000_000,
        limit=60,
    )
    s1 = lax.all_to_all(s1, "hst", split_axis=0, concat_axis=0, tiled=True)
    columns = blocks + peers * cap // BLOCK
    base, bnd = call(
        inner_kernel,
        (shape((nodes, width), F32), shape((peers, cap, width), F32)),
        [SMEM] * 4 + [VMEM] * 4,
        (tile_rows, tile_cols, tile_ids, send_counts, gp, w_neigh, w_self, tile_values),
        [pltpu.VMEM((blocks, BLOCK, width), BF16), pltpu.VMEM((columns, BLOCK, width), F32)],
        flops=350_000_000,
    )
    coords, s2 = call(
        second_kernel,
        (shape((nodes, rank), BF16), shape((peers * wide, BLOCK), BF16)),
        [VMEM] * 5,
        (s1, cross_recv_rows.reshape(groups, BLOCK), feats, lift_part, bnd),
        [pltpu.VMEM((peers * wide, BLOCK), F32)],
        flops=50_000_000,
    )
    s2 = lax.all_to_all(
        s2.reshape(peers, wide, BLOCK), "dev", split_axis=0, concat_axis=0, tiled=True
    )
    slots = recv_rows.reshape(peers, cap)
    recv = jnp.stack(
        [
            jnp.pad(slots, ((0, 0), (at * cap, (2 - at) * cap)), constant_values=-1).reshape(-1)
            for at in range(2)
        ]
    )
    (s3,) = call(third_kernel, (shape((64, 8, BLOCK), BF16),), [VMEM], (s2,), flops=10_000_000)
    s3 = lax.all_to_all(
        s3, both, split_axis=0, concat_axis=0, tiled=True, axis_index_groups=device_groups(("z", "y"))
    )
    (grad_feats,) = call(
        feats_kernel,
        (shape((nodes, width), BF16),),
        [VMEM] * 5,
        (s2.reshape(peers * wide, BLOCK), recv, base, coords, proj.T),
        flops=150_000_000,
    )
    (s4,) = call(
        fourth_kernel,
        (shape((8, 160, BLOCK), BF16),),
        [VMEM],
        (s3,),
        [pltpu.VMEM((512, BLOCK), F32)],
    )
    s4 = lax.all_to_all(
        s4, both, split_axis=0, concat_axis=0, tiled=True,
        axis_index_groups=device_groups(("x", "core")),
    )
    grad_self, grad_neigh, grad_lift, grad_proj = call(
        lambda *refs: last_kernel(norm_scale, *refs),
        (
            shape((width, width), F32),
            shape((width, width), F32),
            shape((rank, width), F32),
            shape((rank, width), F32),
        ),
        [VMEM],
        (s4,),
        [pltpu.VMEM((4, width, BLOCK), F32), pltpu.VMEM((4, rank, BLOCK), F32)],
    )
    return (grad_feats, grad_self, grad_neigh, grad_lift, grad_proj.T)


def solution(mesh):
    both = ("hst", "dev")
    row, cube = P(both, None), P(both, None, None)
    placed = (
        (row,) * 5 + (P(),) * 4 + (cube,) + (row,) * 7 + (cube,) + (row,) + (cube,)
    )
    return jax.shard_map(
        body,
        mesh=mesh,
        in_specs=placed,
        out_specs=(row, P(), P(), P(), P()),
        check_vma=False,
    )
```

```python
import math

import jax
import jax.numpy as jnp
from jax import lax
from jax.experimental import pallas as pl
from jax.experimental.pallas import tpu as pltpu
from jax.sharding import PartitionSpec as P

F32 = jnp.float32
BF16 = jnp.bfloat16
BLOCK = 128

VMEM = pl.BlockSpec(memory_space=pltpu.VMEM)
SMEM = pl.BlockSpec(memory_space=pltpu.SMEM)
HBM = pl.BlockSpec(memory_space=pltpu.HBM)


def dot_nn(a, b):
    return jnp.dot(a, b, preferred_element_type=F32)


def dot_nt(a, b):
    return lax.dot_general(a, b, (((1,), (1,)), ((), ())), preferred_element_type=F32)


def dot_tn(a, b):
    return lax.dot_general(a, b, (((0,), (0,)), ((), ())), preferred_element_type=F32)


def call(kernel, outs, specs, args, scratch=(), flops=0, limit=40):
    nbytes = sum(math.prod(o.shape) * o.dtype.itemsize for o in list(outs) + list(args))
    return pl.pallas_call(
        kernel,
        out_shape=tuple(outs),
        in_specs=specs,
        out_specs=tuple(VMEM for _ in outs),
        scratch_shapes=list(scratch),
        compiler_params=pltpu.CompilerParams(vmem_limit_bytes=limit * 1024 * 1024),
        cost_estimate=pl.CostEstimate(flops=flops, bytes_accessed=nbytes, transcendentals=0),
    )(*args)


def shape(dims, dtype):
    return jax.ShapeDtypeStruct(dims, dtype)


def masked(grad, preact):
    return jnp.where(preact[...].astype(F32) > 0, grad[...].astype(F32), 0.0).astype(BF16)


def first_kernel(
    xrow_in, xcol_in, xid_in, xcount_in, grad_in, preact_in, lift_in, tiles_in, feats_in, agg_in,
    s1_out,
    xrow, xcol, xid, xcount, grad, preact, lift, tiles, feats, agg, cg, acc, sems,
):
    groups = acc.shape[0]
    rank = acc.shape[1]
    pairs = (
        (grad_in, grad), (preact_in, preact), (lift_in, lift), (xrow_in, xrow), (xcol_in, xcol),
        (xid_in, xid), (xcount_in, xcount), (tiles_in, tiles), (feats_in, feats), (agg_in, agg),
    )
    copies = [
        pltpu.make_async_copy(source, target, sems.at[i])
        for i, (source, target) in enumerate(pairs)
    ]
    for copy in copies:
        copy.start()
    for copy in copies:
        copy.wait()
    gp = masked(grad, preact)
    cgt = dot_nt(lift[...], gp).astype(BF16)
    for b in range(cg.shape[0]):
        cg[b] = cgt[:, b * BLOCK : (b + 1) * BLOCK]
    at = rank
    for source in (feats, agg):
        part = dot_tn(source[...], gp).astype(BF16)
        step = part.shape[0] // groups
        for j in range(groups):
            rows = part[j * step : (j + 1) * step]
            s1_out[j, at : at + step, :] = rows[:, :BLOCK]
            s1_out[j, at + step : at + 2 * step, :] = rows[:, BLOCK:]
        at += 2 * step
    acc[...] = jnp.zeros_like(acc)
    for t in range(xrow.shape[1]):
        acc[xcol[0, t]] += dot_nn(cg[xrow[0, t]], tiles[xid[0, t]])
    slot = lax.broadcasted_iota(jnp.int32, (rank, BLOCK), 1)
    for j in range(groups):
        s1_out[j, 0:rank, :] = jnp.where(slot < xcount[0, j], acc[j], 0.0).astype(BF16)


def inner_kernel(
    trow, tcol, tid, counts, grad_out, preact, cross, w_neigh, w_self, tiles,
    base_out, bnd_out, lift_out, ng, acc,
):
    cap = bnd_out.shape[1]
    blocks = ng.shape[0]
    gp = masked(grad_out, preact)
    lift_out[...] = dot_nn(cross[...], gp)
    own = dot_nt(gp, w_self[...])
    grad = dot_nt(gp, w_neigh[...]).astype(BF16)
    for b in range(blocks):
        ng[b] = grad[b * BLOCK : (b + 1) * BLOCK]
    acc[...] = jnp.zeros_like(acc)
    for t in range(trow.shape[1]):
        col = tcol[0, t]
        acc[col] += dot_tn(tiles[tid[0, t]], ng[trow[0, t]])
    for b in range(blocks):
        base_out[b * BLOCK : (b + 1) * BLOCK, :] = own[b * BLOCK : (b + 1) * BLOCK] + acc[b]
    slot = lax.broadcasted_iota(jnp.int32, (cap, acc.shape[2]), 0)
    per_block = BLOCK // cap
    for q in range(bnd_out.shape[0]):
        rows = acc[blocks + q // per_block, (q % per_block) * cap : (q % per_block + 1) * cap, :]
        bnd_out[q] = jnp.where(slot < counts[0, q], rows, 0.0)


def second_kernel(s1, xrecv, feats, lift_part, bnd, coords_out, s2_out, scr):
    groups = s1.shape[0]
    rank = lift_part.shape[0]
    peers = bnd.shape[0]
    cap = bnd.shape[1]
    nodes = feats.shape[0]
    wide = 3 * cap
    row = lax.broadcasted_iota(jnp.int32, (nodes, BLOCK), 0)
    total = None
    for g in range(groups):
        hot = jnp.where(row == xrecv[g : g + 1, :], 1.0, 0.0).astype(BF16)
        term = dot_nt(s1[g, 0:rank, :], hot)
        total = term if total is None else total + term
    coords_t = total.astype(BF16)
    coords_out[...] = total.T.astype(BF16)
    proj_t = dot_nn(coords_t, feats[...])
    summed = s1[0, rank:, :].astype(F32)
    for g in range(1, groups):
        summed = summed + s1[g, rank:, :].astype(F32)
    for q in range(peers):
        scr[q * wide : q * wide + cap, :] = bnd[q, :, :BLOCK]
        scr[q * wide + cap : q * wide + 2 * cap, :] = bnd[q, :, BLOCK:]
    low = proj_t - proj_t.astype(BF16).astype(F32)
    pieces = [summed[:peers], summed[peers:]]
    for value in (proj_t, lift_part[...], low):
        pieces += [value[:, :BLOCK], value[:, BLOCK:]]
    for at, piece in enumerate(pieces):
        scr[pl.ds(2 * cap + at, peers, stride=wide), :] = piece
    s2_out[...] = scr[...].astype(BF16)


def third_kernel(s2, s3_out):
    parts = [s2[q, 16:24, :].astype(F32) for q in range(s2.shape[0])]
    while len(parts) > 1:
        parts = [parts[i] + parts[i + 1] for i in range(0, len(parts), 2)]
    sums = parts[0]
    proj = sums[2:4] + sums[6:8]
    low = proj - proj.astype(BF16).astype(F32)
    share = jnp.concatenate([sums[0:2], proj, sums[4:6], low], axis=0).astype(BF16)
    for j in range(s3_out.shape[0]):
        s3_out[j] = share


def feats_kernel(s2, recv, base, coords, proj_t, out):
    nodes = base.shape[0]
    row = lax.broadcasted_iota(jnp.int32, (nodes, recv.shape[1]), 0)
    for half in range(2):
        lanes = slice(half * BLOCK, (half + 1) * BLOCK)
        hot = jnp.where(row == recv[half : half + 1, :], 1.0, 0.0).astype(BF16)
        value = base[:, lanes] + dot_nn(hot, s2[...]) + dot_nn(coords[...], proj_t[:, lanes])
        out[:, lanes] = value.astype(BF16)


def fourth_kernel(s3, s4_out, scr):
    for j in range(s3.shape[0]):
        scr[j * 8 : (j + 1) * 8, :] = s3[j].astype(F32)
    peers = s3.shape[0]
    side = peers // 8
    pieces = [scr[pl.ds(at, peers, stride=8), :] for at in range(2)]

    def over_groups(at):
        total = scr[pl.ds(at, side, stride=8), :]
        for g in range(1, 8):
            total = total + scr[pl.ds(g * side * 8 + at, side, stride=8), :]
        return total

    for at in range(2):
        pieces.append(over_groups(2 + at) + over_groups(6 + at))
    for at in range(2):
        pieces.append(over_groups(4 + at))
    share = jnp.concatenate(pieces, axis=0).astype(BF16)
    for j in range(s4_out.shape[0]):
        s4_out[j] = share


def last_kernel(norm_scale, s4, self_out, neigh_out, lift_out, proj_out, square, flat):
    groups = 8
    for j in range(s4.shape[0]):
        value = s4[j].astype(F32) * norm_scale
        first = 16 * (j // 2) + j % 2
        for kind in range(2):
            for g in range(groups):
                at = 64 * kind + 8 * g
                square[2 * kind + first // 32, pl.ds(32 * g + first % 32, 8, stride=2), :] = value[
                    at : at + 8
                ]
        for part in range(4):
            at = 128 + 8 * part
            flat[part, pl.ds(first, 8, stride=2), :] = value[at : at + 8]
    for h in range(2):
        lanes = slice(h * BLOCK, (h + 1) * BLOCK)
        self_out[:, lanes] = square[h]
        neigh_out[:, lanes] = square[2 + h]
        proj_out[:, lanes] = flat[h]
        lift_out[:, lanes] = flat[2 + h]


def device_groups(inner):
    sizes = (("z", 8), ("x", 4), ("y", 8), ("core", 2))
    lists = {}
    for z in range(8):
        for x in range(4):
            for y in range(8):
                for core in range(2):
                    place = {"z": z, "x": x, "y": y, "core": core}
                    key = tuple(place[name] for name, _ in sizes if name not in inner)
                    lists.setdefault(key, []).append(((z * 4 + x) * 8 + y) * 2 + core)
    return [lists[key] for key in sorted(lists)]


def body(
    feats,
    grad_out,
    preact,
    neigh_agg,
    cross_coords,
    w_self,
    w_neigh,
    proj,
    lift,
    tile_values,
    tile_rows,
    tile_cols,
    tile_ids,
    cross_rows,
    cross_cols,
    cross_ids,
    send_counts,
    recv_rows,
    cross_counts,
    cross_recv_rows,
):
    nodes, width = feats.shape
    rank = proj.shape[1]
    peers = lax.axis_size("dev")
    groups = lax.axis_size("hst")
    cap = recv_rows.shape[-1]
    blocks = nodes // BLOCK
    norm_scale = 1.0 / math.sqrt(nodes * peers * groups)
    wide = 3 * cap
    both = ("hst", "dev")

    first_args = (
        cross_rows, cross_cols, cross_ids, cross_counts, grad_out, preact, lift, tile_values,
        feats, neigh_agg,
    )
    (s1,) = call(
        first_kernel,
        (shape((groups, rank + 4 * width // groups, BLOCK), BF16),),
        [HBM] * 10,
        first_args,
        [pltpu.SMEM(v.shape, v.dtype) for v in first_args[:4]]
        + [pltpu.VMEM(v.shape, v.dtype) for v in first_args[4:]]
        + [
            pltpu.VMEM((blocks, rank, BLOCK), BF16),
            pltpu.VMEM((groups, rank, BLOCK), F32),
            pltpu.SemaphoreType.DMA((10,)),
        ],
        flops=100_000_000,
        limit=60,
    )
    s1 = lax.all_to_all(s1, "hst", split_axis=0, concat_axis=0, tiled=True)
    slots = recv_rows.reshape(peers, cap)
    recv = jnp.stack(
        [
            jnp.pad(slots, ((0, 0), (at * cap, (2 - at) * cap)), constant_values=-1).reshape(-1)
            for at in range(2)
        ]
    )
    recv, sweep_rows = lax.optimization_barrier((recv, tile_rows))
    columns = blocks + peers * cap // BLOCK
    base, bnd, lift_part = call(
        inner_kernel,
        (
            shape((nodes, width), F32),
            shape((peers, cap, width), F32),
            shape((rank, width), F32),
        ),
        [SMEM] * 4 + [VMEM] * 6,
        (sweep_rows, tile_cols, tile_ids, send_counts, grad_out, preact, cross_coords.T,
         w_neigh, w_self, tile_values),
        [pltpu.VMEM((blocks, BLOCK, width), BF16), pltpu.VMEM((columns, BLOCK, width), F32)],
        flops=350_000_000,
    )
    coords, s2 = call(
        second_kernel,
        (shape((nodes, rank), BF16), shape((peers * wide, BLOCK), BF16)),
        [VMEM] * 5,
        (s1, cross_recv_rows.reshape(groups, BLOCK), feats, lift_part, bnd),
        [pltpu.VMEM((peers * wide, BLOCK), F32)],
        flops=50_000_000,
    )
    s2 = lax.all_to_all(
        s2.reshape(peers, wide, BLOCK), "dev", split_axis=0, concat_axis=0, tiled=True
    )
    (s3,) = call(third_kernel, (shape((64, 8, BLOCK), BF16),), [VMEM], (s2,), flops=10_000_000)
    s3 = lax.all_to_all(
        s3, both, split_axis=0, concat_axis=0, tiled=True, axis_index_groups=device_groups(("z", "y"))
    )
    (grad_feats,) = call(
        feats_kernel,
        (shape((nodes, width), BF16),),
        [VMEM] * 5,
        (s2.reshape(peers * wide, BLOCK), recv, base, coords, proj.T),
        flops=150_000_000,
    )
    s3, grad_feats = lax.optimization_barrier((s3, grad_feats))
    (s4,) = call(
        fourth_kernel,
        (shape((8, 160, BLOCK), BF16),),
        [VMEM],
        (s3,),
        [pltpu.VMEM((512, BLOCK), F32)],
    )
    s4 = lax.all_to_all(
        s4, both, split_axis=0, concat_axis=0, tiled=True,
        axis_index_groups=device_groups(("x", "core")),
    )
    grad_self, grad_neigh, grad_lift, grad_proj = call(
        lambda *refs: last_kernel(norm_scale, *refs),
        (
            shape((width, width), F32),
            shape((width, width), F32),
            shape((rank, width), F32),
            shape((rank, width), F32),
        ),
        [VMEM],
        (s4,),
        [pltpu.VMEM((4, width, BLOCK), F32), pltpu.VMEM((4, rank, BLOCK), F32)],
    )
    return (grad_feats, grad_self, grad_neigh, grad_lift, grad_proj.T)


def solution(mesh):
    both = ("hst", "dev")
    row, cube = P(both, None), P(both, None, None)
    placed = (
        (row,) * 5 + (P(),) * 4 + (cube,) + (row,) * 7 + (cube,) + (row,) + (cube,)
    )
    return jax.shard_map(
        body,
        mesh=mesh,
        in_specs=placed,
        out_specs=(row, P(), P(), P(), P()),
        check_vma=False,
    )
```

```python
import math

import jax
import jax.numpy as jnp
from jax import lax
from jax.experimental import pallas as pl
from jax.experimental.pallas import tpu as pltpu
from jax.sharding import PartitionSpec as P

F32 = jnp.float32
BF16 = jnp.bfloat16
BLOCK = 128

VMEM = pl.BlockSpec(memory_space=pltpu.VMEM)
SMEM = pl.BlockSpec(memory_space=pltpu.SMEM)
HBM = pl.BlockSpec(memory_space=pltpu.HBM)


def dot_nn(a, b):
    return jnp.dot(a, b, preferred_element_type=F32)


def dot_nt(a, b):
    return lax.dot_general(a, b, (((1,), (1,)), ((), ())), preferred_element_type=F32)


def dot_tn(a, b):
    return lax.dot_general(a, b, (((0,), (0,)), ((), ())), preferred_element_type=F32)


def call(kernel, outs, specs, args, scratch=(), flops=0, limit=40):
    nbytes = sum(math.prod(o.shape) * o.dtype.itemsize for o in list(outs) + list(args))
    return pl.pallas_call(
        kernel,
        out_shape=tuple(outs),
        in_specs=specs,
        out_specs=tuple(VMEM for _ in outs),
        scratch_shapes=list(scratch),
        compiler_params=pltpu.CompilerParams(vmem_limit_bytes=limit * 1024 * 1024),
        cost_estimate=pl.CostEstimate(flops=flops, bytes_accessed=nbytes, transcendentals=0),
    )(*args)


def shape(dims, dtype):
    return jax.ShapeDtypeStruct(dims, dtype)


def masked(grad, preact):
    return jnp.where(preact[...].astype(F32) > 0, grad[...].astype(F32), 0.0).astype(BF16)


def first_kernel(
    xrow_in, xcol_in, xid_in, xcount_in, grad_in, preact_in, lift_in, tiles_in, feats_in, agg_in,
    s1_out,
    xrow, xcol, xid, xcount, grad, preact, lift, tiles, feats, agg, cg, acc, sems,
):
    groups = acc.shape[0]
    rank = acc.shape[1]
    pairs = (
        (grad_in, grad), (preact_in, preact), (lift_in, lift), (xrow_in, xrow), (xcol_in, xcol),
        (xid_in, xid), (xcount_in, xcount), (tiles_in, tiles), (feats_in, feats), (agg_in, agg),
    )
    copies = [
        pltpu.make_async_copy(source, target, sems.at[i])
        for i, (source, target) in enumerate(pairs)
    ]
    for copy in copies:
        copy.start()
    for copy in copies:
        copy.wait()
    gp = masked(grad, preact)
    cgt = dot_nt(lift[...], gp).astype(BF16)
    for b in range(cg.shape[0]):
        cg[b] = cgt[:, b * BLOCK : (b + 1) * BLOCK]
    at = rank
    for source in (feats, agg):
        part = dot_tn(source[...], gp).astype(BF16)
        step = part.shape[0] // groups
        for j in range(groups):
            rows = part[j * step : (j + 1) * step]
            s1_out[j, at : at + step, :] = rows[:, :BLOCK]
            s1_out[j, at + step : at + 2 * step, :] = rows[:, BLOCK:]
        at += 2 * step
    acc[...] = jnp.zeros_like(acc)
    for t in range(xrow.shape[1]):
        acc[xcol[0, t]] += dot_nn(cg[xrow[0, t]], tiles[xid[0, t]])
    slot = lax.broadcasted_iota(jnp.int32, (rank, BLOCK), 1)
    for j in range(groups):
        s1_out[j, 0:rank, :] = jnp.where(slot < xcount[0, j], acc[j], 0.0).astype(BF16)


def inner_kernel(
    trow, tcol, tid, counts, grad_out, preact, cross, w_neigh, w_self, tiles,
    base_out, bnd_out, lift_out, ng, acc,
):
    cap = bnd_out.shape[1]
    blocks = ng.shape[0]
    gp = masked(grad_out, preact)
    lift_out[...] = dot_nn(cross[...], gp)
    own = dot_nt(gp, w_self[...])
    grad = dot_nt(gp, w_neigh[...]).astype(BF16)
    for b in range(blocks):
        ng[b] = grad[b * BLOCK : (b + 1) * BLOCK]
    acc[...] = jnp.zeros_like(acc)
    for t in range(trow.shape[1]):
        col = tcol[0, t]
        acc[col] += dot_tn(tiles[tid[0, t]], ng[trow[0, t]])
    for b in range(blocks):
        base_out[b * BLOCK : (b + 1) * BLOCK, :] = own[b * BLOCK : (b + 1) * BLOCK] + acc[b]
    slot = lax.broadcasted_iota(jnp.int32, (cap, acc.shape[2]), 0)
    per_block = BLOCK // cap
    for q in range(bnd_out.shape[0]):
        rows = acc[blocks + q // per_block, (q % per_block) * cap : (q % per_block + 1) * cap, :]
        bnd_out[q] = jnp.where(slot < counts[0, q], rows, 0.0)


def second_kernel(s1, xrecv, feats, lift_part, bnd, coords_out, s2_out, scr):
    groups = s1.shape[0]
    rank = lift_part.shape[0]
    peers = bnd.shape[0]
    cap = bnd.shape[1]
    nodes = feats.shape[0]
    wide = 2 * cap + 6
    row = lax.broadcasted_iota(jnp.int32, (nodes, BLOCK), 0)
    total = None
    for g in range(groups):
        hot = jnp.where(row == xrecv[g : g + 1, :], 1.0, 0.0).astype(BF16)
        term = dot_nt(s1[g, 0:rank, :], hot)
        total = term if total is None else total + term
    coords_t = total.astype(BF16)
    coords_out[...] = total.T.astype(BF16)
    proj_t = dot_nn(coords_t, feats[...])
    summed = s1[0, rank:, :].astype(F32)
    for g in range(1, groups):
        summed = summed + s1[g, rank:, :].astype(F32)
    for q in range(peers):
        scr[q * wide : q * wide + cap, :] = bnd[q, :, :BLOCK]
        scr[q * wide + cap : q * wide + 2 * cap, :] = bnd[q, :, BLOCK:]
    pieces = [summed[:peers], summed[peers:]]
    for value in (proj_t, lift_part[...]):
        pieces += [value[:, :BLOCK], value[:, BLOCK:]]
    for at, piece in enumerate(pieces):
        scr[pl.ds(2 * cap + at, peers, stride=wide), :] = piece
    s2_out[...] = scr[...].astype(BF16)


def third_kernel(s2, s3_out, scr):
    peers = 64
    wide = s2.shape[0] // peers
    scr[...] = s2[...].astype(F32)
    sums = [
        jnp.sum(scr[pl.ds(wide - 6 + at, peers, stride=wide), :], axis=0, keepdims=True)
        for at in range(6)
    ]
    share = jnp.concatenate(sums * 8, axis=0).astype(BF16)
    for j in range(8):
        s3_out[48 * j : 48 * (j + 1), :] = share


def feats_kernel(s2, recv, base, coords, proj_t, out):
    nodes = base.shape[0]
    row = lax.broadcasted_iota(jnp.int32, (nodes, recv.shape[1]), 0)
    for half in range(2):
        lanes = slice(half * BLOCK, (half + 1) * BLOCK)
        hot = jnp.where(row == recv[half : half + 1, :], 1.0, 0.0).astype(BF16)
        value = base[:, lanes] + dot_nn(hot, s2[...]) + dot_nn(coords[...], proj_t[:, lanes])
        out[:, lanes] = value.astype(BF16)


def fourth_kernel(s3, s4_out, scr):
    scr[...] = s3[...].astype(F32)
    peers = s3.shape[0] // 6
    side = peers // 8
    pieces = [scr[pl.ds(at, peers, stride=6), :] for at in range(2)]
    for at in range(2, 6):
        total = scr[pl.ds(at, side, stride=6), :]
        for g in range(1, 8):
            total = total + scr[pl.ds(g * side * 6 + at, side, stride=6), :]
        pieces.append(total)
    share = jnp.concatenate(pieces, axis=0).astype(BF16)
    for j in range(s4_out.shape[0]):
        s4_out[j] = share


def last_kernel(norm_scale, s4, self_out, neigh_out, lift_out, proj_out, square, flat):
    groups = 8
    for j in range(s4.shape[0]):
        value = s4[j].astype(F32) * norm_scale
        first = 16 * (j // 2) + j % 2
        for kind in range(2):
            for g in range(groups):
                at = 64 * kind + 8 * g
                square[2 * kind + first // 32, pl.ds(32 * g + first % 32, 8, stride=2), :] = value[
                    at : at + 8
                ]
        for part in range(4):
            at = 128 + 8 * part
            flat[part, pl.ds(first, 8, stride=2), :] = value[at : at + 8]
    for h in range(2):
        lanes = slice(h * BLOCK, (h + 1) * BLOCK)
        self_out[:, lanes] = square[h]
        neigh_out[:, lanes] = square[2 + h]
        proj_out[:, lanes] = flat[h]
        lift_out[:, lanes] = flat[2 + h]


def device_groups(inner):
    sizes = (("z", 8), ("x", 4), ("y", 8), ("core", 2))
    lists = {}
    for z in range(8):
        for x in range(4):
            for y in range(8):
                for core in range(2):
                    place = {"z": z, "x": x, "y": y, "core": core}
                    key = tuple(place[name] for name, _ in sizes if name not in inner)
                    lists.setdefault(key, []).append(((z * 4 + x) * 8 + y) * 2 + core)
    return [lists[key] for key in sorted(lists)]


def body(
    feats,
    grad_out,
    preact,
    neigh_agg,
    cross_coords,
    w_self,
    w_neigh,
    proj,
    lift,
    tile_values,
    tile_rows,
    tile_cols,
    tile_ids,
    cross_rows,
    cross_cols,
    cross_ids,
    send_counts,
    recv_rows,
    cross_counts,
    cross_recv_rows,
):
    nodes, width = feats.shape
    rank = proj.shape[1]
    peers = lax.axis_size("dev")
    groups = lax.axis_size("hst")
    cap = recv_rows.shape[-1]
    blocks = nodes // BLOCK
    norm_scale = 1.0 / math.sqrt(nodes * peers * groups)
    wide = 2 * cap + 6
    both = ("hst", "dev")

    first_args = (
        cross_rows, cross_cols, cross_ids, cross_counts, grad_out, preact, lift, tile_values,
        feats, neigh_agg,
    )
    (s1,) = call(
        first_kernel,
        (shape((groups, rank + 4 * width // groups, BLOCK), BF16),),
        [HBM] * 10,
        first_args,
        [pltpu.SMEM(v.shape, v.dtype) for v in first_args[:4]]
        + [pltpu.VMEM(v.shape, v.dtype) for v in first_args[4:]]
        + [
            pltpu.VMEM((blocks, rank, BLOCK), BF16),
            pltpu.VMEM((groups, rank, BLOCK), F32),
            pltpu.SemaphoreType.DMA((10,)),
        ],
        flops=100_000_000,
        limit=60,
    )
    s1 = lax.all_to_all(s1, "hst", split_axis=0, concat_axis=0, tiled=True)
    slots = recv_rows.reshape(peers, cap)
    recv = jnp.stack(
        [
            jnp.pad(slots, ((0, 0), (at * cap, wide - (at + 1) * cap)), constant_values=-1).reshape(-1)
            for at in range(2)
        ]
    )
    recv, sweep_rows = lax.optimization_barrier((recv, tile_rows))
    columns = blocks + peers * cap // BLOCK
    base, bnd, lift_part = call(
        inner_kernel,
        (
            shape((nodes, width), F32),
            shape((peers, cap, width), F32),
            shape((rank, width), F32),
        ),
        [SMEM] * 4 + [VMEM] * 6,
        (sweep_rows, tile_cols, tile_ids, send_counts, grad_out, preact, cross_coords.T,
         w_neigh, w_self, tile_values),
        [pltpu.VMEM((blocks, BLOCK, width), BF16), pltpu.VMEM((columns, BLOCK, width), F32)],
        flops=350_000_000,
    )
    coords, s2 = call(
        second_kernel,
        (shape((nodes, rank), BF16), shape((peers * wide, BLOCK), BF16)),
        [VMEM] * 5,
        (s1, cross_recv_rows.reshape(groups, BLOCK), feats, lift_part, bnd),
        [pltpu.VMEM((peers * wide, BLOCK), F32)],
        flops=50_000_000,
    )
    s2 = lax.all_to_all(
        s2.reshape(peers * wide // 2, 2, BLOCK), "dev", split_axis=0, concat_axis=0, tiled=True
    ).reshape(peers * wide, BLOCK)
    (s3,) = call(
        third_kernel,
        (shape((64 * 6, BLOCK), BF16),),
        [VMEM],
        (s2,),
        [pltpu.VMEM((peers * wide, BLOCK), F32)],
        flops=10_000_000,
    )
    s3 = lax.all_to_all(
        s3.reshape(64 * 3, 2, BLOCK), both, split_axis=0, concat_axis=0, tiled=True,
        axis_index_groups=device_groups(("z", "y")),
    ).reshape(64 * 6, BLOCK)
    (grad_feats,) = call(
        feats_kernel,
        (shape((nodes, width), BF16),),
        [VMEM] * 5,
        (s2, recv, base, coords, proj.T),
        flops=150_000_000,
    )
    s3, grad_feats = lax.optimization_barrier((s3, grad_feats))
    (s4,) = call(
        fourth_kernel,
        (shape((8, 160, BLOCK), BF16),),
        [VMEM],
        (s3,),
        [pltpu.VMEM((64 * 6, BLOCK), F32)],
    )
    s4 = lax.all_to_all(
        s4, both, split_axis=0, concat_axis=0, tiled=True,
        axis_index_groups=device_groups(("x", "core")),
    )
    grad_self, grad_neigh, grad_lift, grad_proj = call(
        lambda *refs: last_kernel(norm_scale, *refs),
        (
            shape((width, width), F32),
            shape((width, width), F32),
            shape((rank, width), F32),
            shape((rank, width), F32),
        ),
        [VMEM],
        (s4,),
        [pltpu.VMEM((4, width, BLOCK), F32), pltpu.VMEM((4, rank, BLOCK), F32)],
    )
    return (grad_feats, grad_self, grad_neigh, grad_lift, grad_proj.T)


def solution(mesh):
    both = ("hst", "dev")
    row, cube = P(both, None), P(both, None, None)
    placed = (
        (row,) * 5 + (P(),) * 4 + (cube,) + (row,) * 7 + (cube,) + (row,) + (cube,)
    )
    return jax.shard_map(
        body,
        mesh=mesh,
        in_specs=placed,
        out_specs=(row, P(), P(), P(), P()),
        check_vma=False,
    )
```

```python
import math

import jax
import jax.numpy as jnp
from jax import lax
from jax.experimental import pallas as pl
from jax.experimental.pallas import tpu as pltpu
from jax.sharding import PartitionSpec as P

F32 = jnp.float32
BF16 = jnp.bfloat16
BLOCK = 128

VMEM = pl.BlockSpec(memory_space=pltpu.VMEM)
SMEM = pl.BlockSpec(memory_space=pltpu.SMEM)
HBM = pl.BlockSpec(memory_space=pltpu.HBM)


def dot_nn(a, b):
    return jnp.dot(a, b, preferred_element_type=F32)


def dot_nt(a, b):
    return lax.dot_general(a, b, (((1,), (1,)), ((), ())), preferred_element_type=F32)


def dot_tn(a, b):
    return lax.dot_general(a, b, (((0,), (0,)), ((), ())), preferred_element_type=F32)


def call(kernel, outs, specs, args, scratch=(), flops=0, limit=40):
    nbytes = sum(math.prod(o.shape) * o.dtype.itemsize for o in list(outs) + list(args))
    return pl.pallas_call(
        kernel,
        out_shape=tuple(outs),
        in_specs=specs,
        out_specs=tuple(VMEM for _ in outs),
        scratch_shapes=list(scratch),
        compiler_params=pltpu.CompilerParams(vmem_limit_bytes=limit * 1024 * 1024),
        cost_estimate=pl.CostEstimate(flops=flops, bytes_accessed=nbytes, transcendentals=0),
    )(*args)


def shape(dims, dtype):
    return jax.ShapeDtypeStruct(dims, dtype)


def masked(grad, preact):
    return jnp.where(preact[...].astype(F32) > 0, grad[...].astype(F32), 0.0).astype(BF16)


def first_kernel(
    xrow_in, xcol_in, xid_in, xcount_in, grad_in, preact_in, lift_in, tiles_in, feats_in, agg_in, coords_in,
    s1_out,
    xrow, xcol, xid, xcount, grad, preact, lift, tiles, feats, agg, coords, cg, acc, sems,
):
    groups = acc.shape[0]
    rank = acc.shape[1]
    pairs = (
        (grad_in, grad), (preact_in, preact), (lift_in, lift), (xrow_in, xrow), (xcol_in, xcol),
        (xid_in, xid), (xcount_in, xcount), (tiles_in, tiles), (feats_in, feats), (agg_in, agg),
        (coords_in, coords),
    )
    copies = [
        pltpu.make_async_copy(source, target, sems.at[i])
        for i, (source, target) in enumerate(pairs)
    ]
    for copy in copies:
        copy.start()
    for copy in copies:
        copy.wait()
    gp = masked(grad, preact)
    cgt = dot_nt(lift[...], gp).astype(BF16)
    for b in range(cg.shape[0]):
        cg[b] = cgt[:, b * BLOCK : (b + 1) * BLOCK]
    at = rank
    for source in (feats, agg):
        part = dot_tn(source[...], gp).astype(BF16)
        step = part.shape[0] // groups
        for j in range(groups):
            rows = part[j * step : (j + 1) * step]
            s1_out[j, at : at + step, :] = rows[:, :BLOCK]
            s1_out[j, at + step : at + 2 * step, :] = rows[:, BLOCK:]
        at += 2 * step
    part = dot_nn(coords[...], gp)
    step = rank // groups
    for j in range(groups):
        rows = part[j * step : (j + 1) * step]
        halves = jnp.concatenate([rows[:, :BLOCK], rows[:, BLOCK:]], axis=0)
        s1_out[j, at : at + 2 * step, :] = halves.astype(BF16)
    acc[...] = jnp.zeros_like(acc)
    for t in range(xrow.shape[1]):
        acc[xcol[0, t]] += dot_nn(cg[xrow[0, t]], tiles[xid[0, t]])
    slot = lax.broadcasted_iota(jnp.int32, (rank, BLOCK), 1)
    for j in range(groups):
        s1_out[j, 0:rank, :] = jnp.where(slot < xcount[0, j], acc[j], 0.0).astype(BF16)


def inner_kernel(
    trow, tcol, tid, counts, grad_out, preact, w_neigh, w_self, tiles,
    base_out, bnd_out, ng, acc,
):
    cap = bnd_out.shape[1]
    blocks = ng.shape[0]
    gp = masked(grad_out, preact)
    own = dot_nt(gp, w_self[...])
    grad = dot_nt(gp, w_neigh[...]).astype(BF16)
    for b in range(blocks):
        ng[b] = grad[b * BLOCK : (b + 1) * BLOCK]
    acc[...] = jnp.zeros_like(acc)
    for t in range(trow.shape[1]):
        col = tcol[0, t]
        acc[col] += dot_tn(tiles[tid[0, t]], ng[trow[0, t]])
    for b in range(blocks):
        base_out[b * BLOCK : (b + 1) * BLOCK, :] = own[b * BLOCK : (b + 1) * BLOCK] + acc[b]
    slot = lax.broadcasted_iota(jnp.int32, (cap, acc.shape[2]), 0)
    per_block = BLOCK // cap
    for q in range(bnd_out.shape[0]):
        rows = acc[blocks + q // per_block, (q % per_block) * cap : (q % per_block + 1) * cap, :]
        bnd_out[q] = jnp.where(slot < counts[0, q], rows, 0.0)


def second_kernel(s1, xrecv, feats, bnd, coords_out, s2_out, scr):
    groups = s1.shape[0]
    rank = coords_out.shape[1]
    peers = bnd.shape[0]
    cap = bnd.shape[1]
    nodes = feats.shape[0]
    wide = 2 * cap + 10
    row = lax.broadcasted_iota(jnp.int32, (nodes, BLOCK), 0)
    total = None
    for g in range(groups):
        hot = jnp.where(row == xrecv[g : g + 1, :], 1.0, 0.0).astype(BF16)
        term = dot_nt(s1[g, 0:rank, :], hot)
        total = term if total is None else total + term
    coords_t = total.astype(BF16)
    coords_out[...] = total.T.astype(BF16)
    proj_t = dot_nn(coords_t, feats[...])
    summed = s1[0, rank:, :].astype(F32)
    for g in range(1, groups):
        summed = summed + s1[g, rank:, :].astype(F32)
    for q in range(peers):
        scr[q * wide : q * wide + cap, :] = bnd[q, :, :BLOCK]
        scr[q * wide + cap : q * wide + 2 * cap, :] = bnd[q, :, BLOCK:]
    share = peers // 2
    pieces = [summed[at * share : (at + 1) * share] for at in range(4)]
    for h in range(2):
        for at in range(2):
            pieces.append(proj_t[at * share : (at + 1) * share, h * BLOCK : (h + 1) * BLOCK])
    lift_rows = summed[4 * share :]
    pieces += [jnp.concatenate([lift_rows, lift_rows], axis=0), jnp.zeros((share, BLOCK), F32)]
    for at, piece in enumerate(pieces):
        twice = [piece[8 * (i // 2) : 8 * (i // 2) + 8] for i in range(peers // 8)]
        scr[pl.ds(2 * cap + at, peers, stride=wide), :] = jnp.concatenate(twice, axis=0)
    s2_out[...] = scr[...].astype(BF16)


def third_kernel(s2, s3_out, scr):
    peers = 64
    wide = s2.shape[0] // peers
    scr[...] = s2[...].astype(F32)
    sums = [
        jnp.sum(scr[pl.ds(wide - 10 + at, peers, stride=wide), :], axis=0, keepdims=True)
        for at in range(9)
    ] + [jnp.zeros((1, BLOCK), F32)]
    share = jnp.concatenate(sums * 8, axis=0).astype(BF16)
    for j in range(4):
        s3_out[80 * j : 80 * (j + 1), :] = share


def feats_kernel(s2, recv, base, coords, proj_t, out):
    nodes = base.shape[0]
    row = lax.broadcasted_iota(jnp.int32, (nodes, recv.shape[1]), 0)
    for half in range(2):
        lanes = slice(half * BLOCK, (half + 1) * BLOCK)
        hot = jnp.where(row == recv[half : half + 1, :], 1.0, 0.0).astype(BF16)
        value = base[:, lanes] + dot_nn(hot, s2[...]) + dot_nn(coords[...], proj_t[:, lanes])
        out[:, lanes] = value.astype(BF16)


def fourth_kernel(s3, s4_out, scr):
    scr[...] = s3[...].astype(F32)
    peers = s3.shape[0] // 10
    side = peers // 8
    pieces = [scr[pl.ds(at, peers, stride=10), :] for at in range(4)]
    for at in range(4, 8):
        total = scr[pl.ds(at, side, stride=10), :]
        for g in range(1, 8):
            total = total + scr[pl.ds(g * side * 10 + at, side, stride=10), :]
        pieces.append(total)
    pieces.append(scr[pl.ds(8, peers, stride=10), :])
    share = jnp.concatenate(pieces, axis=0).astype(BF16)
    for j in range(s4_out.shape[0]):
        s4_out[j] = share


def last_kernel(norm_scale, s4, self_out, neigh_out, lift_out, proj_out, square, flat):
    for j in range(s4.shape[0]):
        value = s4[j].astype(F32) * norm_scale
        first = 8 * (j // 2) + j % 2
        for kind in range(4):
            for g in range(8):
                at = 32 * kind + 4 * g
                square[kind, pl.ds(32 * g + first, 4, stride=2), :] = value[at : at + 4]
        for part in range(4):
            at = 128 + 4 * part
            flat[part // 2, pl.ds(32 * (part % 2) + first, 4, stride=2), :] = value[at : at + 4]
        if j < 4:
            for g in range(8):
                at = 144 + 4 * g
                flat[2 + j // 2, pl.ds(8 * g + j % 2, 4, stride=2), :] = value[at : at + 4]
    for h in range(2):
        lanes = slice(h * BLOCK, (h + 1) * BLOCK)
        self_out[:, lanes] = square[h]
        neigh_out[:, lanes] = square[2 + h]
        proj_out[:, lanes] = flat[h]
        lift_out[:, lanes] = flat[2 + h]


def device_groups(inner):
    sizes = (("z", 8), ("x", 4), ("side", 2), ("y", 4), ("core", 2))
    lists = {}
    for device in range(512):
        place, rest = {}, device
        for name, size in reversed(sizes):
            place[name], rest = rest % size, rest // size
        key = tuple(place[name] for name, _ in sizes if name not in inner)
        lists.setdefault(key, []).append(device)
    return [lists[key] for key in sorted(lists)]


def body(
    feats,
    grad_out,
    preact,
    neigh_agg,
    cross_coords,
    w_self,
    w_neigh,
    proj,
    lift,
    tile_values,
    tile_rows,
    tile_cols,
    tile_ids,
    cross_rows,
    cross_cols,
    cross_ids,
    send_counts,
    recv_rows,
    cross_counts,
    cross_recv_rows,
):
    nodes, width = feats.shape
    rank = proj.shape[1]
    peers = lax.axis_size("dev")
    groups = lax.axis_size("hst")
    cap = recv_rows.shape[-1]
    blocks = nodes // BLOCK
    norm_scale = 1.0 / math.sqrt(nodes * peers * groups)
    wide = 2 * cap + 10
    both = ("hst", "dev")

    first_args = (
        cross_rows, cross_cols, cross_ids, cross_counts, grad_out, preact, lift, tile_values,
        feats, neigh_agg, cross_coords.T,
    )
    (s1,) = call(
        first_kernel,
        (shape((groups, rank + 4 * width // groups + 2 * rank // groups, BLOCK), BF16),),
        [HBM] * 11,
        first_args,
        [pltpu.SMEM(v.shape, v.dtype) for v in first_args[:4]]
        + [pltpu.VMEM(v.shape, v.dtype) for v in first_args[4:]]
        + [
            pltpu.VMEM((blocks, rank, BLOCK), BF16),
            pltpu.VMEM((groups, rank, BLOCK), F32),
            pltpu.SemaphoreType.DMA((11,)),
        ],
        flops=100_000_000,
        limit=60,
    )
    s1 = lax.all_to_all(s1, "hst", split_axis=0, concat_axis=0, tiled=True)
    slots = recv_rows.reshape(peers, cap)
    recv = jnp.stack(
        [
            jnp.pad(slots, ((0, 0), (at * cap, wide - (at + 1) * cap)), constant_values=-1).reshape(-1)
            for at in range(2)
        ]
    )
    recv, sweep_rows = lax.optimization_barrier((recv, tile_rows))
    columns = blocks + peers * cap // BLOCK
    base, bnd = call(
        inner_kernel,
        (
            shape((nodes, width), F32),
            shape((peers, cap, width), F32),
        ),
        [SMEM] * 4 + [VMEM] * 5,
        (sweep_rows, tile_cols, tile_ids, send_counts, grad_out, preact,
         w_neigh, w_self, tile_values),
        [pltpu.VMEM((blocks, BLOCK, width), BF16), pltpu.VMEM((columns, BLOCK, width), F32)],
        flops=350_000_000,
    )
    coords, s2 = call(
        second_kernel,
        (shape((nodes, rank), BF16), shape((peers * wide, BLOCK), BF16)),
        [VMEM] * 4,
        (s1, cross_recv_rows.reshape(groups, BLOCK), feats, bnd),
        [pltpu.VMEM((peers * wide, BLOCK), F32)],
        flops=50_000_000,
    )
    s2 = lax.all_to_all(
        s2.reshape(peers * wide // 2, 2, BLOCK), "dev", split_axis=0, concat_axis=0, tiled=True
    ).reshape(peers * wide, BLOCK)
    (s3,) = call(
        third_kernel,
        (shape((32 * 10, BLOCK), BF16),),
        [VMEM],
        (s2,),
        [pltpu.VMEM((peers * wide, BLOCK), F32)],
        flops=10_000_000,
    )
    s3 = lax.all_to_all(
        s3.reshape(32 * 5, 2, BLOCK), both, split_axis=0, concat_axis=0, tiled=True,
        axis_index_groups=device_groups(("z", "y")),
    ).reshape(32 * 10, BLOCK)
    (grad_feats,) = call(
        feats_kernel,
        (shape((nodes, width), BF16),),
        [VMEM] * 5,
        (s2, recv, base, coords, proj.T),
        flops=150_000_000,
    )
    (s4,) = call(
        fourth_kernel,
        (shape((8, 176, BLOCK), BF16),),
        [VMEM],
        (s3,),
        [pltpu.VMEM((32 * 10, BLOCK), F32)],
    )
    s4 = lax.all_to_all(
        s4, both, split_axis=0, concat_axis=0, tiled=True,
        axis_index_groups=device_groups(("x", "core")),
    )
    grad_self, grad_neigh, grad_lift, grad_proj = call(
        lambda *refs: last_kernel(norm_scale, *refs),
        (
            shape((width, width), F32),
            shape((width, width), F32),
            shape((rank, width), F32),
            shape((rank, width), F32),
        ),
        [VMEM],
        (s4,),
        [pltpu.VMEM((4, width, BLOCK), F32), pltpu.VMEM((4, rank, BLOCK), F32)],
    )
    return (grad_feats, grad_self, grad_neigh, grad_lift, grad_proj.T)


def solution(mesh):
    both = ("hst", "dev")
    row, cube = P(both, None), P(both, None, None)
    placed = (
        (row,) * 5 + (P(),) * 4 + (cube,) + (row,) * 7 + (cube,) + (row,) + (cube,)
    )
    return jax.shard_map(
        body,
        mesh=mesh,
        in_specs=placed,
        out_specs=(row, P(), P(), P(), P()),
        check_vma=False,
    )
```

```python
import math

import jax
import jax.numpy as jnp
from jax import lax
from jax.experimental import pallas as pl
from jax.experimental.pallas import tpu as pltpu
from jax.sharding import PartitionSpec as P

F32 = jnp.float32
BF16 = jnp.bfloat16
BLOCK = 128
ROOM = 32

VMEM = pl.BlockSpec(memory_space=pltpu.VMEM)
SMEM = pl.BlockSpec(memory_space=pltpu.SMEM)
HBM = pl.BlockSpec(memory_space=pltpu.HBM)


def dot_nn(a, b):
    return jnp.dot(a, b, preferred_element_type=F32)


def dot_nt(a, b):
    return lax.dot_general(a, b, (((1,), (1,)), ((), ())), preferred_element_type=F32)


def dot_tn(a, b):
    return lax.dot_general(a, b, (((0,), (0,)), ((), ())), preferred_element_type=F32)


def call(kernel, outs, specs, args, scratch=(), flops=0, limit=40):
    nbytes = sum(math.prod(o.shape) * o.dtype.itemsize for o in list(outs) + list(args))
    return pl.pallas_call(
        kernel,
        out_shape=tuple(outs),
        in_specs=specs,
        out_specs=tuple(VMEM for _ in outs),
        scratch_shapes=list(scratch),
        compiler_params=pltpu.CompilerParams(vmem_limit_bytes=limit * 1024 * 1024),
        cost_estimate=pl.CostEstimate(flops=flops, bytes_accessed=nbytes, transcendentals=0),
    )(*args)


def shape(dims, dtype):
    return jax.ShapeDtypeStruct(dims, dtype)


def masked(grad, preact):
    return jnp.where(preact[...].astype(F32) > 0, grad[...].astype(F32), 0.0).astype(BF16)


def first_kernel(
    xrow_in, xcol_in, xid_in, xcount_in, grad_in, preact_in, lift_in, tiles_in, feats_in, agg_in, coords_in,
    s1_out,
    xrow, xcol, xid, xcount, grad, preact, lift, tiles, feats, agg, coords, cg, acc, sems,
):
    groups = acc.shape[0]
    rank = acc.shape[1]
    pairs = (
        (grad_in, grad), (preact_in, preact), (lift_in, lift), (xrow_in, xrow), (xcol_in, xcol),
        (xid_in, xid), (xcount_in, xcount), (tiles_in, tiles), (feats_in, feats), (agg_in, agg),
        (coords_in, coords),
    )
    copies = [
        pltpu.make_async_copy(source, target, sems.at[i])
        for i, (source, target) in enumerate(pairs)
    ]
    for copy in copies:
        copy.start()
    for copy in copies:
        copy.wait()
    gp = masked(grad, preact)
    cgt = dot_nt(lift[...], gp).astype(BF16)
    for b in range(cg.shape[0]):
        cg[b] = cgt[:, b * BLOCK : (b + 1) * BLOCK]
    at = rank
    for source in (feats, agg):
        part = dot_tn(source[...], gp).astype(BF16)
        step = part.shape[0] // groups
        for j in range(groups):
            rows = part[j * step : (j + 1) * step]
            s1_out[j, at : at + step, :] = rows[:, :BLOCK]
            s1_out[j, at + step : at + 2 * step, :] = rows[:, BLOCK:]
        at += 2 * step
    part = dot_nn(coords[...], gp)
    step = rank // groups
    for j in range(groups):
        rows = part[j * step : (j + 1) * step]
        halves = jnp.concatenate([rows[:, :BLOCK], rows[:, BLOCK:]], axis=0)
        s1_out[j, at : at + 2 * step, :] = halves.astype(BF16)
    acc[...] = jnp.zeros_like(acc)
    for t in range(xrow.shape[1]):
        acc[xcol[0, t]] += dot_nn(cg[xrow[0, t]], tiles[xid[0, t]])
    slot = lax.broadcasted_iota(jnp.int32, (rank, BLOCK), 1)
    for j in range(groups):
        s1_out[j, 0:rank, :] = jnp.where(slot < xcount[0, j], acc[j], 0.0).astype(BF16)


def inner_kernel(
    trow, tcol, tid, counts, grad_out, preact, w_neigh, w_self, tiles,
    base_out, bnd_out, ng, acc,
):
    cap = bnd_out.shape[1]
    blocks = ng.shape[0]
    gp = masked(grad_out, preact)
    own = dot_nt(gp, w_self[...])
    grad = dot_nt(gp, w_neigh[...]).astype(BF16)
    for b in range(blocks):
        ng[b] = grad[b * BLOCK : (b + 1) * BLOCK]
    acc[...] = jnp.zeros_like(acc)
    for t in range(trow.shape[1]):
        col = tcol[0, t]
        acc[col] += dot_tn(tiles[tid[0, t]], ng[trow[0, t]])
    for b in range(blocks):
        base_out[b * BLOCK : (b + 1) * BLOCK, :] = own[b * BLOCK : (b + 1) * BLOCK] + acc[b]
    slot = lax.broadcasted_iota(jnp.int32, (cap, acc.shape[2]), 0)
    per_block = BLOCK // cap
    for q in range(bnd_out.shape[0]):
        rows = acc[blocks + q // per_block, (q % per_block) * cap : (q % per_block + 1) * cap, :]
        bnd_out[q] = jnp.where(slot < counts[0, q], rows, 0.0)


def second_kernel(s1, xrecv, feats, bnd, coords_out, s2_out, scr):
    groups = s1.shape[0]
    rank = coords_out.shape[1]
    peers = bnd.shape[0]
    cap = bnd.shape[1]
    nodes = feats.shape[0]
    wide = 2 * cap + 10
    row = lax.broadcasted_iota(jnp.int32, (nodes, BLOCK), 0)
    total = None
    for g in range(groups):
        hot = jnp.where(row == xrecv[g : g + 1, :], 1.0, 0.0).astype(BF16)
        term = dot_nt(s1[g, 0:rank, :], hot)
        total = term if total is None else total + term
    coords_t = total.astype(BF16)
    coords_out[...] = total.T.astype(BF16)
    proj_t = dot_nn(coords_t, feats[...])
    summed = s1[0, rank:, :].astype(F32)
    for g in range(1, groups):
        summed = summed + s1[g, rank:, :].astype(F32)
    for q in range(peers):
        scr[q * wide : q * wide + cap, :] = bnd[q, :, :BLOCK]
        scr[q * wide + cap : q * wide + 2 * cap, :] = bnd[q, :, BLOCK:]
    share = peers // 2
    pieces = [summed[at * share : (at + 1) * share] for at in range(4)]
    for h in range(2):
        for at in range(2):
            pieces.append(proj_t[at * share : (at + 1) * share, h * BLOCK : (h + 1) * BLOCK])
    lift_rows = summed[4 * share :]
    pieces += [jnp.concatenate([lift_rows, lift_rows], axis=0), jnp.zeros((share, BLOCK), F32)]
    for at, piece in enumerate(pieces):
        twice = [piece[8 * (i // 2) : 8 * (i // 2) + 8] for i in range(peers // 8)]
        scr[pl.ds(2 * cap + at, peers, stride=wide), :] = jnp.concatenate(twice, axis=0)
    s2_out[...] = scr[: s2_out.shape[0]].astype(BF16)


def third_kernel(s2, s3_out, scr):
    peers = 64
    wide = s2.shape[0] // peers
    scr[: s2.shape[0], :] = s2[...].astype(F32)
    sums = [
        jnp.sum(scr[pl.ds(wide - 10 + at, peers, stride=wide), :], axis=0, keepdims=True)
        for at in range(9)
    ] + [jnp.zeros((1, BLOCK), F32)]
    share = jnp.concatenate(sums * 8, axis=0).astype(BF16)
    for j in range(4):
        s3_out[80 * j : 80 * (j + 1), :] = share


def feats_kernel(s2, recv, base, coords, proj_t, out):
    nodes = base.shape[0]
    row = lax.broadcasted_iota(jnp.int32, (nodes, recv.shape[1]), 0)
    for half in range(2):
        lanes = slice(half * BLOCK, (half + 1) * BLOCK)
        hot = jnp.where(row == recv[half : half + 1, :], 1.0, 0.0).astype(BF16)
        value = base[:, lanes] + dot_nn(hot, s2[...]) + dot_nn(coords[...], proj_t[:, lanes])
        out[:, lanes] = value.astype(BF16)


def fourth_kernel(s3, s4_out, scr):
    scr[: s3.shape[0], :] = s3[...].astype(F32)
    peers = s3.shape[0] // 10
    side = peers // 8
    pieces = [scr[pl.ds(at, peers, stride=10), :] for at in range(4)]
    for at in range(4, 8):
        total = scr[pl.ds(at, side, stride=10), :]
        for g in range(1, 8):
            total = total + scr[pl.ds(g * side * 10 + at, side, stride=10), :]
        pieces.append(total)
    pieces.append(scr[pl.ds(8, peers, stride=10), :])
    share = jnp.concatenate(pieces, axis=0).astype(BF16)
    for j in range(s4_out.shape[0]):
        s4_out[j] = share


def last_kernel(norm_scale, s4, self_out, neigh_out, lift_out, proj_out, square, flat):
    for j in range(s4.shape[0]):
        value = s4[j].astype(F32) * norm_scale
        first = 8 * (j // 2) + j % 2
        for kind in range(4):
            for g in range(8):
                at = 32 * kind + 4 * g
                square[kind, pl.ds(32 * g + first, 4, stride=2), :] = value[at : at + 4]
        for part in range(4):
            at = 128 + 4 * part
            flat[part // 2, pl.ds(32 * (part % 2) + first, 4, stride=2), :] = value[at : at + 4]
        if j < 4:
            for g in range(8):
                at = 144 + 4 * g
                flat[2 + j // 2, pl.ds(8 * g + j % 2, 4, stride=2), :] = value[at : at + 4]
    for h in range(2):
        lanes = slice(h * BLOCK, (h + 1) * BLOCK)
        self_out[:, lanes] = square[h, : self_out.shape[0]]
        neigh_out[:, lanes] = square[2 + h, : neigh_out.shape[0]]
        proj_out[:, lanes] = flat[h, : proj_out.shape[0]]
        lift_out[:, lanes] = flat[2 + h, : lift_out.shape[0]]


def device_groups(inner):
    sizes = (("z", 8), ("x", 4), ("side", 2), ("y", 4), ("core", 2))
    lists = {}
    for device in range(512):
        place, rest = {}, device
        for name, size in reversed(sizes):
            place[name], rest = rest % size, rest // size
        key = tuple(place[name] for name, _ in sizes if name not in inner)
        lists.setdefault(key, []).append(device)
    return [lists[key] for key in sorted(lists)]


def body(
    feats,
    grad_out,
    preact,
    neigh_agg,
    cross_coords,
    w_self,
    w_neigh,
    proj,
    lift,
    tile_values,
    tile_rows,
    tile_cols,
    tile_ids,
    cross_rows,
    cross_cols,
    cross_ids,
    send_counts,
    recv_rows,
    cross_counts,
    cross_recv_rows,
):
    nodes, width = feats.shape
    rank = proj.shape[1]
    peers = lax.axis_size("dev")
    groups = lax.axis_size("hst")
    cap = recv_rows.shape[-1]
    blocks = nodes // BLOCK
    norm_scale = 1.0 / math.sqrt(nodes * peers * groups)
    wide = 2 * cap + 10
    both = ("hst", "dev")

    first_args = (
        cross_rows, cross_cols, cross_ids, cross_counts, grad_out, preact, lift, tile_values,
        feats, neigh_agg, cross_coords.T,
    )
    (s1,) = call(
        first_kernel,
        (shape((groups, rank + 4 * width // groups + 2 * rank // groups, BLOCK), BF16),),
        [HBM] * 11,
        first_args,
        [pltpu.SMEM(v.shape, v.dtype) for v in first_args[:4]]
        + [pltpu.VMEM(v.shape, v.dtype) for v in first_args[4:]]
        + [
            pltpu.VMEM((blocks, rank, BLOCK), BF16),
            pltpu.VMEM((groups, rank, BLOCK), F32),
            pltpu.SemaphoreType.DMA((11,)),
        ],
        flops=100_000_000,
        limit=60,
    )
    s1 = lax.all_to_all(s1, "hst", split_axis=0, concat_axis=0, tiled=True)
    slots = recv_rows.reshape(peers, cap)
    recv = jnp.stack(
        [
            jnp.pad(slots, ((0, 0), (at * cap, wide - (at + 1) * cap)), constant_values=-1).reshape(-1)
            for at in range(2)
        ]
    )
    recv, sweep_rows = lax.optimization_barrier((recv, tile_rows))
    columns = blocks + peers * cap // BLOCK
    base, bnd = call(
        inner_kernel,
        (
            shape((nodes, width), F32),
            shape((peers, cap, width), F32),
        ),
        [SMEM] * 4 + [VMEM] * 5,
        (sweep_rows, tile_cols, tile_ids, send_counts, grad_out, preact,
         w_neigh, w_self, tile_values),
        [pltpu.VMEM((blocks, BLOCK, width), BF16), pltpu.VMEM((columns, BLOCK, width), F32)],
        flops=350_000_000,
    )
    coords, s2 = call(
        second_kernel,
        (shape((nodes, rank), BF16), shape((peers * wide, BLOCK), BF16)),
        [VMEM] * 4,
        (s1, cross_recv_rows.reshape(groups, BLOCK), feats, bnd),
        [pltpu.VMEM((peers * wide + ROOM, BLOCK), F32)],
        flops=50_000_000,
    )
    s2 = lax.all_to_all(
        s2.reshape(peers * wide // 2, 2, BLOCK), "dev", split_axis=0, concat_axis=0, tiled=True
    ).reshape(peers * wide, BLOCK)
    (s3,) = call(
        third_kernel,
        (shape((32 * 10, BLOCK), BF16),),
        [VMEM],
        (s2,),
        [pltpu.VMEM((peers * wide + ROOM, BLOCK), F32)],
        flops=10_000_000,
    )
    s3 = lax.all_to_all(
        s3.reshape(32 * 5, 2, BLOCK), both, split_axis=0, concat_axis=0, tiled=True,
        axis_index_groups=device_groups(("z", "y")),
    ).reshape(32 * 10, BLOCK)
    (grad_feats,) = call(
        feats_kernel,
        (shape((nodes, width), BF16),),
        [VMEM] * 5,
        (s2, recv, base, coords, proj.T),
        flops=150_000_000,
    )
    (s4,) = call(
        fourth_kernel,
        (shape((8, 176, BLOCK), BF16),),
        [VMEM],
        (s3,),
        [pltpu.VMEM((32 * 10 + 2 * ROOM, BLOCK), F32)],
    )
    s4 = lax.all_to_all(
        s4, both, split_axis=0, concat_axis=0, tiled=True,
        axis_index_groups=device_groups(("x", "core")),
    )
    grad_self, grad_neigh, grad_lift, grad_proj = call(
        lambda *refs: last_kernel(norm_scale, *refs),
        (
            shape((width, width), F32),
            shape((width, width), F32),
            shape((rank, width), F32),
            shape((rank, width), F32),
        ),
        [VMEM],
        (s4,),
        [pltpu.VMEM((4, width + ROOM, BLOCK), F32), pltpu.VMEM((4, rank + ROOM, BLOCK), F32)],
    )
    return (grad_feats, grad_self, grad_neigh, grad_lift, grad_proj.T)


def solution(mesh):
    both = ("hst", "dev")
    row, cube = P(both, None), P(both, None, None)
    placed = (
        (row,) * 5 + (P(),) * 4 + (cube,) + (row,) * 7 + (cube,) + (row,) + (cube,)
    )
    return jax.shard_map(
        body,
        mesh=mesh,
        in_specs=placed,
        out_specs=(row, P(), P(), P(), P()),
        check_vma=False,
    )
```

```python
import math

import jax
import jax.numpy as jnp
from jax import lax
from jax.experimental import pallas as pl
from jax.experimental.pallas import tpu as pltpu
from jax.sharding import PartitionSpec as P

F32 = jnp.float32
BF16 = jnp.bfloat16
BLOCK = 128
ROOM = 32

VMEM = pl.BlockSpec(memory_space=pltpu.VMEM)
SMEM = pl.BlockSpec(memory_space=pltpu.SMEM)
HBM = pl.BlockSpec(memory_space=pltpu.HBM)


def dot_nn(a, b):
    return jnp.dot(a, b, preferred_element_type=F32)


def dot_nt(a, b):
    return lax.dot_general(a, b, (((1,), (1,)), ((), ())), preferred_element_type=F32)


def dot_tn(a, b):
    return lax.dot_general(a, b, (((0,), (0,)), ((), ())), preferred_element_type=F32)


def call(kernel, outs, specs, args, scratch=(), flops=0, limit=40):
    nbytes = sum(math.prod(o.shape) * o.dtype.itemsize for o in list(outs) + list(args))
    return pl.pallas_call(
        kernel,
        out_shape=tuple(outs),
        in_specs=specs,
        out_specs=tuple(VMEM for _ in outs),
        scratch_shapes=list(scratch),
        compiler_params=pltpu.CompilerParams(vmem_limit_bytes=limit * 1024 * 1024),
        cost_estimate=pl.CostEstimate(flops=flops, bytes_accessed=nbytes, transcendentals=0),
    )(*args)


def shape(dims, dtype):
    return jax.ShapeDtypeStruct(dims, dtype)


def masked(grad, preact):
    return jnp.where(preact[...].astype(F32) > 0, grad[...].astype(F32), 0.0).astype(BF16)


def first_kernel(
    xrow_in, xcol_in, xid_in, xcount_in, grad_in, preact_in, lift_in, tiles_in, feats_in, agg_in, coords_in,
    s1_out,
    xrow, xcol, xid, xcount, grad, preact, lift, tiles, feats, agg, coords, cg, acc, sems,
):
    groups = acc.shape[0]
    rank = acc.shape[1]
    pairs = (
        (grad_in, grad), (preact_in, preact), (lift_in, lift), (xrow_in, xrow), (xcol_in, xcol),
        (xid_in, xid), (xcount_in, xcount), (tiles_in, tiles), (feats_in, feats), (agg_in, agg),
        (coords_in, coords),
    )
    copies = [
        pltpu.make_async_copy(source, target, sems.at[i])
        for i, (source, target) in enumerate(pairs)
    ]
    for copy in copies:
        copy.start()
    for copy in copies:
        copy.wait()
    gp = masked(grad, preact)
    cgt = dot_nt(lift[...], gp).astype(BF16)
    for b in range(cg.shape[0]):
        cg[b] = cgt[:, b * BLOCK : (b + 1) * BLOCK]
    at = rank
    for source in (feats, agg):
        part = dot_tn(source[...], gp).astype(BF16)
        step = part.shape[0] // groups
        for j in range(groups):
            rows = part[j * step : (j + 1) * step]
            s1_out[j, at : at + step, :] = rows[:, :BLOCK]
            s1_out[j, at + step : at + 2 * step, :] = rows[:, BLOCK:]
        at += 2 * step
    part = dot_nn(coords[...], gp)
    step = rank // groups
    for j in range(groups):
        rows = part[j * step : (j + 1) * step]
        halves = jnp.concatenate([rows[:, :BLOCK], rows[:, BLOCK:]], axis=0)
        s1_out[j, at : at + 2 * step, :] = halves.astype(BF16)
    acc[...] = jnp.zeros_like(acc)
    for t in range(xrow.shape[1]):
        acc[xcol[0, t]] += dot_nn(cg[xrow[0, t]], tiles[xid[0, t]])
    slot = lax.broadcasted_iota(jnp.int32, (rank, BLOCK), 1)
    for j in range(groups):
        s1_out[j, 0:rank, :] = jnp.where(slot < xcount[0, j], acc[j], 0.0).astype(BF16)


def inner_kernel(
    trow, tcol, tid, counts, grad_out, preact, w_neigh, w_self, tiles,
    base_out, bnd_out, ng, acc,
):
    cap = bnd_out.shape[1]
    blocks = ng.shape[0]
    gp = masked(grad_out, preact)
    own = dot_nt(gp, w_self[...])
    grad = dot_nt(gp, w_neigh[...]).astype(BF16)
    for b in range(blocks):
        ng[b] = grad[b * BLOCK : (b + 1) * BLOCK]
    acc[...] = jnp.zeros_like(acc)
    for t in range(trow.shape[1]):
        col = tcol[0, t]
        acc[col] += dot_tn(tiles[tid[0, t]], ng[trow[0, t]])
    for b in range(blocks):
        base_out[b * BLOCK : (b + 1) * BLOCK, :] = own[b * BLOCK : (b + 1) * BLOCK] + acc[b]
    slot = lax.broadcasted_iota(jnp.int32, (cap, acc.shape[2]), 0)
    per_block = BLOCK // cap
    for q in range(bnd_out.shape[0]):
        rows = acc[blocks + q // per_block, (q % per_block) * cap : (q % per_block + 1) * cap, :]
        bnd_out[q] = jnp.where(slot < counts[0, q], rows, 0.0)


def second_kernel(s1, xrecv, feats, bnd, coords_out, s2_out, scr):
    groups = s1.shape[0]
    rank = coords_out.shape[1]
    peers = bnd.shape[0]
    cap = bnd.shape[1]
    nodes = feats.shape[0]
    wide = 2 * cap + 10
    row = lax.broadcasted_iota(jnp.int32, (nodes, BLOCK), 0)
    total = None
    for g in range(groups):
        hot = jnp.where(row == xrecv[g : g + 1, :], 1.0, 0.0).astype(BF16)
        term = dot_nt(s1[g, 0:rank, :], hot)
        total = term if total is None else total + term
    coords_t = total.astype(BF16)
    coords_out[...] = total.T.astype(BF16)
    proj_t = dot_nn(coords_t, feats[...])
    summed = s1[0, rank:, :].astype(F32)
    for g in range(1, groups):
        summed = summed + s1[g, rank:, :].astype(F32)
    for q in range(peers):
        scr[q * wide : q * wide + cap, :] = bnd[q, :, :BLOCK]
        scr[q * wide + cap : q * wide + 2 * cap, :] = bnd[q, :, BLOCK:]
    share = peers // 2
    pieces = [summed[at * share : (at + 1) * share] for at in range(4)]
    for h in range(2):
        for at in range(2):
            pieces.append(proj_t[at * share : (at + 1) * share, h * BLOCK : (h + 1) * BLOCK])
    lift_rows = summed[4 * share :]
    side = BLOCK // 2
    lift_rows = jnp.concatenate([lift_rows[:, :side], lift_rows[:, side:]], axis=0)
    lift_rows = jnp.concatenate([lift_rows, jnp.zeros((share, side), F32)], axis=1)
    pieces += [lift_rows, jnp.zeros((share, BLOCK), F32)]
    for at, piece in enumerate(pieces):
        twice = [piece[8 * (i // 2) : 8 * (i // 2) + 8] for i in range(peers // 8)]
        scr[pl.ds(2 * cap + at, peers, stride=wide), :] = jnp.concatenate(twice, axis=0)
    s2_out[...] = scr[: s2_out.shape[0]].astype(BF16)


def third_kernel(s2, s3_out, scr):
    peers = 64
    wide = s2.shape[0] // peers
    scr[: s2.shape[0], :] = s2[...].astype(F32)
    sums = [
        jnp.sum(scr[pl.ds(wide - 10 + at, peers, stride=wide), :], axis=0, keepdims=True)
        for at in range(9)
    ] + [jnp.zeros((1, BLOCK), F32)]
    share = jnp.concatenate(sums * 8, axis=0).astype(BF16)
    for j in range(4):
        s3_out[80 * j : 80 * (j + 1), :] = share


def feats_kernel(s2, recv, base, coords, proj_t, out):
    nodes = base.shape[0]
    row = lax.broadcasted_iota(jnp.int32, (nodes, recv.shape[1]), 0)
    for half in range(2):
        lanes = slice(half * BLOCK, (half + 1) * BLOCK)
        hot = jnp.where(row == recv[half : half + 1, :], 1.0, 0.0).astype(BF16)
        value = base[:, lanes] + dot_nn(hot, s2[...]) + dot_nn(coords[...], proj_t[:, lanes])
        out[:, lanes] = value.astype(BF16)


def fourth_kernel(s3, s4_out, scr):
    scr[: s3.shape[0], :] = s3[...].astype(F32)
    peers = s3.shape[0] // 10
    side = peers // 8
    pieces = [scr[pl.ds(at, peers, stride=10), :] for at in range(4)]
    for at in range(4, 8):
        total = scr[pl.ds(at, side, stride=10), :]
        for g in range(1, 8):
            total = total + scr[pl.ds(g * side * 10 + at, side, stride=10), :]
        pieces.append(total)
    lift = scr[pl.ds(8, peers, stride=10), :]
    pieces.append(
        jnp.concatenate(
            [lift[: peers // 2, : BLOCK // 2], lift[peers // 2 :, : BLOCK // 2]], axis=1
        )
    )
    share = jnp.concatenate(pieces, axis=0).astype(BF16)
    for j in range(s4_out.shape[0]):
        s4_out[j] = share


def last_kernel(norm_scale, s4, self_out, neigh_out, lift_out, proj_out, square, flat):
    values = [s4[j].astype(F32) * norm_scale for j in range(s4.shape[0])]
    for j, value in enumerate(values):
        first = 8 * (j // 2) + j % 2
        for kind in range(4):
            for g in range(8):
                at = 32 * kind + 4 * g
                square[kind, pl.ds(32 * g + first, 4, stride=2), :] = value[at : at + 4]
        for part in range(4):
            at = 128 + 4 * part
            flat[part // 2, pl.ds(32 * (part % 2) + first, 4, stride=2), :] = value[at : at + 4]
        if j < 4:
            for part in range(2):
                lanes = slice(part * BLOCK // 2, (part + 1) * BLOCK // 2)
                lift = jnp.concatenate([value[144:, lanes], values[j + 4][144:, lanes]], axis=1)
                for g in range(4):
                    at = 8 * (4 * part + g) + j % 2
                    flat[2 + j // 2, pl.ds(at, 4, stride=2), :] = lift[4 * g : 4 * g + 4]
    for h in range(2):
        lanes = slice(h * BLOCK, (h + 1) * BLOCK)
        self_out[:, lanes] = square[h, : self_out.shape[0]]
        neigh_out[:, lanes] = square[2 + h, : neigh_out.shape[0]]
        proj_out[:, lanes] = flat[h, : proj_out.shape[0]]
        lift_out[:, lanes] = flat[2 + h, : lift_out.shape[0]]


def device_groups(inner):
    sizes = (("z", 8), ("x", 4), ("side", 2), ("y", 4), ("core", 2))
    lists = {}
    for device in range(512):
        place, rest = {}, device
        for name, size in reversed(sizes):
            place[name], rest = rest % size, rest // size
        key = tuple(place[name] for name, _ in sizes if name not in inner)
        lists.setdefault(key, []).append(device)
    return [lists[key] for key in sorted(lists)]


def body(
    feats,
    grad_out,
    preact,
    neigh_agg,
    cross_coords,
    w_self,
    w_neigh,
    proj,
    lift,
    tile_values,
    tile_rows,
    tile_cols,
    tile_ids,
    cross_rows,
    cross_cols,
    cross_ids,
    send_counts,
    recv_rows,
    cross_counts,
    cross_recv_rows,
):
    nodes, width = feats.shape
    rank = proj.shape[1]
    peers = lax.axis_size("dev")
    groups = lax.axis_size("hst")
    cap = recv_rows.shape[-1]
    blocks = nodes // BLOCK
    norm_scale = 1.0 / math.sqrt(nodes * peers * groups)
    wide = 2 * cap + 10
    both = ("hst", "dev")

    first_args = (
        cross_rows, cross_cols, cross_ids, cross_counts, grad_out, preact, lift, tile_values,
        feats, neigh_agg, cross_coords.T,
    )
    (s1,) = call(
        first_kernel,
        (shape((groups, rank + 4 * width // groups + 2 * rank // groups, BLOCK), BF16),),
        [HBM] * 11,
        first_args,
        [pltpu.SMEM(v.shape, v.dtype) for v in first_args[:4]]
        + [pltpu.VMEM(v.shape, v.dtype) for v in first_args[4:]]
        + [
            pltpu.VMEM((blocks, rank, BLOCK), BF16),
            pltpu.VMEM((groups, rank, BLOCK), F32),
            pltpu.SemaphoreType.DMA((11,)),
        ],
        flops=100_000_000,
        limit=60,
    )
    s1 = lax.all_to_all(s1, "hst", split_axis=0, concat_axis=0, tiled=True)
    slots = recv_rows.reshape(peers, cap)
    recv = jnp.stack(
        [
            jnp.pad(slots, ((0, 0), (at * cap, wide - (at + 1) * cap)), constant_values=-1).reshape(-1)
            for at in range(2)
        ]
    )
    recv, sweep_rows = lax.optimization_barrier((recv, tile_rows))
    columns = blocks + peers * cap // BLOCK
    base, bnd = call(
        inner_kernel,
        (
            shape((nodes, width), F32),
            shape((peers, cap, width), F32),
        ),
        [SMEM] * 4 + [VMEM] * 5,
        (sweep_rows, tile_cols, tile_ids, send_counts, grad_out, preact,
         w_neigh, w_self, tile_values),
        [pltpu.VMEM((blocks, BLOCK, width), BF16), pltpu.VMEM((columns, BLOCK, width), F32)],
        flops=350_000_000,
    )
    coords, s2 = call(
        second_kernel,
        (shape((nodes, rank), BF16), shape((peers * wide, BLOCK), BF16)),
        [VMEM] * 4,
        (s1, cross_recv_rows.reshape(groups, BLOCK), feats, bnd),
        [pltpu.VMEM((peers * wide + ROOM, BLOCK), F32)],
        flops=50_000_000,
    )
    s2 = lax.all_to_all(
        s2.reshape(peers * wide // 2, 2, BLOCK), "dev", split_axis=0, concat_axis=0, tiled=True
    ).reshape(peers * wide, BLOCK)
    (s3,) = call(
        third_kernel,
        (shape((32 * 10, BLOCK), BF16),),
        [VMEM],
        (s2,),
        [pltpu.VMEM((peers * wide + ROOM, BLOCK), F32)],
        flops=10_000_000,
    )
    s3 = lax.all_to_all(
        s3.reshape(32 * 5, 2, BLOCK), both, split_axis=0, concat_axis=0, tiled=True,
        axis_index_groups=device_groups(("z", "y")),
    ).reshape(32 * 10, BLOCK)
    (grad_feats,) = call(
        feats_kernel,
        (shape((nodes, width), BF16),),
        [VMEM] * 5,
        (s2, recv, base, coords, proj.T),
        flops=150_000_000,
    )
    (s4,) = call(
        fourth_kernel,
        (shape((8, 160, BLOCK), BF16),),
        [VMEM],
        (s3,),
        [pltpu.VMEM((32 * 10 + 2 * ROOM, BLOCK), F32)],
    )
    s4 = lax.all_to_all(
        s4, both, split_axis=0, concat_axis=0, tiled=True,
        axis_index_groups=device_groups(("x", "core")),
    )
    grad_self, grad_neigh, grad_lift, grad_proj = call(
        lambda *refs: last_kernel(norm_scale, *refs),
        (
            shape((width, width), F32),
            shape((width, width), F32),
            shape((rank, width), F32),
            shape((rank, width), F32),
        ),
        [VMEM],
        (s4,),
        [pltpu.VMEM((4, width + ROOM, BLOCK), F32), pltpu.VMEM((4, rank + ROOM, BLOCK), F32)],
    )
    return (grad_feats, grad_self, grad_neigh, grad_lift, grad_proj.T)


def solution(mesh):
    both = ("hst", "dev")
    row, cube = P(both, None), P(both, None, None)
    placed = (
        (row,) * 5 + (P(),) * 4 + (cube,) + (row,) * 7 + (cube,) + (row,) + (cube,)
    )
    return jax.shard_map(
        body,
        mesh=mesh,
        in_specs=placed,
        out_specs=(row, P(), P(), P(), P()),
        check_vma=False,
    )
```

```python
import math

import jax
import jax.numpy as jnp
from jax import lax
from jax.experimental import pallas as pl
from jax.experimental.pallas import tpu as pltpu
from jax.sharding import PartitionSpec as P

F32 = jnp.float32
BF16 = jnp.bfloat16
BLOCK = 128
ROOM = 32

VMEM = pl.BlockSpec(memory_space=pltpu.VMEM)
SMEM = pl.BlockSpec(memory_space=pltpu.SMEM)
HBM = pl.BlockSpec(memory_space=pltpu.HBM)


def dot_nn(a, b):
    return jnp.dot(a, b, preferred_element_type=F32)


def dot_nt(a, b):
    return lax.dot_general(a, b, (((1,), (1,)), ((), ())), preferred_element_type=F32)


def dot_tn(a, b):
    return lax.dot_general(a, b, (((0,), (0,)), ((), ())), preferred_element_type=F32)


def call(kernel, outs, specs, args, scratch=(), flops=0, limit=16):
    nbytes = sum(math.prod(o.shape) * o.dtype.itemsize for o in list(outs) + list(args))
    return pl.pallas_call(
        kernel,
        out_shape=tuple(outs),
        in_specs=specs,
        out_specs=tuple(VMEM for _ in outs),
        scratch_shapes=list(scratch),
        compiler_params=pltpu.CompilerParams(vmem_limit_bytes=limit * 1024 * 1024),
        cost_estimate=pl.CostEstimate(flops=flops, bytes_accessed=nbytes, transcendentals=0),
    )(*args)


def shape(dims, dtype):
    return jax.ShapeDtypeStruct(dims, dtype)


def masked(grad, preact):
    return jnp.where(preact[...].astype(F32) > 0, grad[...].astype(F32), 0.0).astype(BF16)


def first_kernel(
    xrow_in, xcol_in, xid_in, xcount_in, grad_in, preact_in, lift_in, tiles_in, feats_in, agg_in, coords_in,
    s1_out,
    xrow, xcol, xid, xcount, grad, preact, lift, tiles, feats, agg, coords, cg, acc, sems,
):
    groups = acc.shape[0]
    rank = acc.shape[1]
    pairs = (
        (grad_in, grad), (preact_in, preact), (lift_in, lift), (xrow_in, xrow), (xcol_in, xcol),
        (xid_in, xid), (xcount_in, xcount), (tiles_in, tiles), (feats_in, feats), (agg_in, agg),
        (coords_in, coords),
    )
    copies = [
        pltpu.make_async_copy(source, target, sems.at[i])
        for i, (source, target) in enumerate(pairs)
    ]
    for copy in copies:
        copy.start()
    for copy in copies:
        copy.wait()
    gp = masked(grad, preact)
    cgt = dot_nt(lift[...], gp).astype(BF16)
    for b in range(cg.shape[0]):
        cg[b] = cgt[:, b * BLOCK : (b + 1) * BLOCK]
    at = rank
    for source in (feats, agg):
        part = dot_tn(source[...], gp).astype(BF16)
        step = part.shape[0] // groups
        for j in range(groups):
            rows = part[j * step : (j + 1) * step]
            s1_out[j, at : at + step, :] = rows[:, :BLOCK]
            s1_out[j, at + step : at + 2 * step, :] = rows[:, BLOCK:]
        at += 2 * step
    part = dot_nn(coords[...], gp)
    step = rank // groups
    for j in range(groups):
        rows = part[j * step : (j + 1) * step]
        halves = jnp.concatenate([rows[:, :BLOCK], rows[:, BLOCK:]], axis=0)
        s1_out[j, at : at + 2 * step, :] = halves.astype(BF16)
    acc[...] = jnp.zeros_like(acc)
    for t in range(xrow.shape[1]):
        acc[xcol[0, t]] += dot_nn(cg[xrow[0, t]], tiles[xid[0, t]])
    slot = lax.broadcasted_iota(jnp.int32, (rank, BLOCK), 1)
    for j in range(groups):
        s1_out[j, 0:rank, :] = jnp.where(slot < xcount[0, j], acc[j], 0.0).astype(BF16)


def inner_kernel(
    trow, tcol, tid, counts, grad_out, preact, w_neigh, w_self, tiles,
    base_out, bnd_out, ng, acc,
):
    cap = bnd_out.shape[1]
    blocks = ng.shape[0]
    gp = masked(grad_out, preact)
    own = dot_nt(gp, w_self[...])
    grad = dot_nt(gp, w_neigh[...]).astype(BF16)
    for b in range(blocks):
        ng[b] = grad[b * BLOCK : (b + 1) * BLOCK]
    acc[...] = jnp.zeros_like(acc)
    for t in range(trow.shape[1]):
        col = tcol[0, t]
        acc[col] += dot_tn(tiles[tid[0, t]], ng[trow[0, t]])
    for b in range(blocks):
        base_out[b * BLOCK : (b + 1) * BLOCK, :] = own[b * BLOCK : (b + 1) * BLOCK] + acc[b]
    slot = lax.broadcasted_iota(jnp.int32, (cap, acc.shape[2]), 0)
    per_block = BLOCK // cap
    for q in range(bnd_out.shape[0]):
        rows = acc[blocks + q // per_block, (q % per_block) * cap : (q % per_block + 1) * cap, :]
        bnd_out[q] = jnp.where(slot < counts[0, q], rows, 0.0)


def second_kernel(s1, xrecv, feats, bnd, coords_out, s2_out, scr):
    groups = s1.shape[0]
    rank = coords_out.shape[1]
    peers = bnd.shape[0]
    cap = bnd.shape[1]
    nodes = feats.shape[0]
    wide = 2 * cap + 10
    row = lax.broadcasted_iota(jnp.int32, (nodes, BLOCK), 0)
    total = None
    for g in range(groups):
        hot = jnp.where(row == xrecv[g : g + 1, :], 1.0, 0.0).astype(BF16)
        term = dot_nt(s1[g, 0:rank, :], hot)
        total = term if total is None else total + term
    coords_t = total.astype(BF16)
    coords_out[...] = total.T.astype(BF16)
    proj_t = dot_nn(coords_t, feats[...])
    summed = s1[0, rank:, :].astype(F32)
    for g in range(1, groups):
        summed = summed + s1[g, rank:, :].astype(F32)
    for q in range(peers):
        scr[q * wide : q * wide + cap, :] = bnd[q, :, :BLOCK]
        scr[q * wide + cap : q * wide + 2 * cap, :] = bnd[q, :, BLOCK:]
    share = peers // 2
    pieces = [summed[at * share : (at + 1) * share] for at in range(4)]
    for h in range(2):
        for at in range(2):
            pieces.append(proj_t[at * share : (at + 1) * share, h * BLOCK : (h + 1) * BLOCK])
    lift_rows = summed[4 * share :]
    side = BLOCK // 2
    lift_rows = jnp.concatenate([lift_rows[:, :side], lift_rows[:, side:]], axis=0)
    lift_rows = jnp.concatenate([lift_rows, jnp.zeros((share, side), F32)], axis=1)
    pieces += [lift_rows, jnp.zeros((share, BLOCK), F32)]
    for at, piece in enumerate(pieces):
        twice = [piece[8 * (i // 2) : 8 * (i // 2) + 8] for i in range(peers // 8)]
        scr[pl.ds(2 * cap + at, peers, stride=wide), :] = jnp.concatenate(twice, axis=0)
    s2_out[...] = scr[: s2_out.shape[0]].astype(BF16)


def third_kernel(s2, s3_out, scr):
    peers = 64
    wide = s2.shape[0] // peers
    scr[: s2.shape[0], :] = s2[...].astype(F32)
    sums = [
        jnp.sum(scr[pl.ds(wide - 10 + at, peers, stride=wide), :], axis=0, keepdims=True)
        for at in range(9)
    ] + [jnp.zeros((1, BLOCK), F32)]
    share = jnp.concatenate(sums * 8, axis=0).astype(BF16)
    for j in range(4):
        s3_out[80 * j : 80 * (j + 1), :] = share


def feats_kernel(s2, recv, base, coords, proj_t, out):
    nodes = base.shape[0]
    row = lax.broadcasted_iota(jnp.int32, (nodes, recv.shape[1]), 0)
    for half in range(2):
        lanes = slice(half * BLOCK, (half + 1) * BLOCK)
        hot = jnp.where(row == recv[half : half + 1, :], 1.0, 0.0).astype(BF16)
        value = base[:, lanes] + dot_nn(hot, s2[...]) + dot_nn(coords[...], proj_t[:, lanes])
        out[:, lanes] = value.astype(BF16)


def fourth_kernel(s3, s4_out, scr):
    scr[: s3.shape[0], :] = s3[...].astype(F32)
    peers = s3.shape[0] // 10
    side = peers // 8
    pieces = [scr[pl.ds(at, peers, stride=10), :] for at in range(4)]
    for at in range(4, 8):
        total = scr[pl.ds(at, side, stride=10), :]
        for g in range(1, 8):
            total = total + scr[pl.ds(g * side * 10 + at, side, stride=10), :]
        pieces.append(total)
    lift = scr[pl.ds(8, peers, stride=10), :]
    pieces.append(
        jnp.concatenate(
            [lift[: peers // 2, : BLOCK // 2], lift[peers // 2 :, : BLOCK // 2]], axis=1
        )
    )
    share = jnp.concatenate(pieces, axis=0).astype(BF16)
    for j in range(s4_out.shape[0]):
        s4_out[j] = share


def last_kernel(norm_scale, s4, self_out, neigh_out, lift_out, proj_out, square, flat):
    values = [s4[j].astype(F32) * norm_scale for j in range(s4.shape[0])]
    for j, value in enumerate(values):
        first = 8 * (j // 2) + j % 2
        for kind in range(4):
            for g in range(8):
                at = 32 * kind + 4 * g
                square[kind, pl.ds(32 * g + first, 4, stride=2), :] = value[at : at + 4]
        for part in range(4):
            at = 128 + 4 * part
            flat[part // 2, pl.ds(32 * (part % 2) + first, 4, stride=2), :] = value[at : at + 4]
        if j < 4:
            for part in range(2):
                lanes = slice(part * BLOCK // 2, (part + 1) * BLOCK // 2)
                lift = jnp.concatenate([value[144:, lanes], values[j + 4][144:, lanes]], axis=1)
                for g in range(4):
                    at = 8 * (4 * part + g) + j % 2
                    flat[2 + j // 2, pl.ds(at, 4, stride=2), :] = lift[4 * g : 4 * g + 4]
    for h in range(2):
        lanes = slice(h * BLOCK, (h + 1) * BLOCK)
        self_out[:, lanes] = square[h, : self_out.shape[0]]
        neigh_out[:, lanes] = square[2 + h, : neigh_out.shape[0]]
        proj_out[:, lanes] = flat[h, : proj_out.shape[0]]
        lift_out[:, lanes] = flat[2 + h, : lift_out.shape[0]]


def device_groups(inner):
    sizes = (("z", 8), ("x", 4), ("side", 2), ("y", 4), ("core", 2))
    lists = {}
    for device in range(512):
        place, rest = {}, device
        for name, size in reversed(sizes):
            place[name], rest = rest % size, rest // size
        key = tuple(place[name] for name, _ in sizes if name not in inner)
        lists.setdefault(key, []).append(device)
    return [lists[key] for key in sorted(lists)]


def body(
    feats,
    grad_out,
    preact,
    neigh_agg,
    cross_coords,
    w_self,
    w_neigh,
    proj,
    lift,
    tile_values,
    tile_rows,
    tile_cols,
    tile_ids,
    cross_rows,
    cross_cols,
    cross_ids,
    send_counts,
    recv_rows,
    cross_counts,
    cross_recv_rows,
):
    nodes, width = feats.shape
    rank = proj.shape[1]
    peers = lax.axis_size("dev")
    groups = lax.axis_size("hst")
    cap = recv_rows.shape[-1]
    blocks = nodes // BLOCK
    norm_scale = 1.0 / math.sqrt(nodes * peers * groups)
    wide = 2 * cap + 10
    both = ("hst", "dev")

    first_args = (
        cross_rows, cross_cols, cross_ids, cross_counts, grad_out, preact, lift, tile_values,
        feats, neigh_agg, cross_coords.T,
    )
    (s1,) = call(
        first_kernel,
        (shape((groups, rank + 4 * width // groups + 2 * rank // groups, BLOCK), BF16),),
        [HBM] * 11,
        first_args,
        [pltpu.SMEM(v.shape, v.dtype) for v in first_args[:4]]
        + [pltpu.VMEM(v.shape, v.dtype) for v in first_args[4:]]
        + [
            pltpu.VMEM((blocks, rank, BLOCK), BF16),
            pltpu.VMEM((groups, rank, BLOCK), F32),
            pltpu.SemaphoreType.DMA((11,)),
        ],
        flops=100_000_000,
        limit=60,
    )
    s1 = lax.all_to_all(s1, "hst", split_axis=0, concat_axis=0, tiled=True)
    slots = recv_rows.reshape(peers, cap)
    recv = jnp.stack(
        [
            jnp.pad(slots, ((0, 0), (at * cap, wide - (at + 1) * cap)), constant_values=-1).reshape(-1)
            for at in range(2)
        ]
    )
    recv, sweep_rows = lax.optimization_barrier((recv, tile_rows))
    columns = blocks + peers * cap // BLOCK
    base, bnd = call(
        inner_kernel,
        (
            shape((nodes, width), F32),
            shape((peers, cap, width), F32),
        ),
        [SMEM] * 4 + [VMEM] * 5,
        (sweep_rows, tile_cols, tile_ids, send_counts, grad_out, preact,
         w_neigh, w_self, tile_values),
        [pltpu.VMEM((blocks, BLOCK, width), BF16), pltpu.VMEM((columns, BLOCK, width), F32)],
        flops=350_000_000,
    )
    coords, s2 = call(
        second_kernel,
        (shape((nodes, rank), BF16), shape((peers * wide, BLOCK), BF16)),
        [VMEM] * 4,
        (s1, cross_recv_rows.reshape(groups, BLOCK), feats, bnd),
        [pltpu.VMEM((peers * wide + ROOM, BLOCK), F32)],
        flops=50_000_000,
    )
    s2 = lax.all_to_all(
        s2.reshape(peers * wide // 2, 2, BLOCK), "dev", split_axis=0, concat_axis=0, tiled=True
    ).reshape(peers * wide, BLOCK)
    (s3,) = call(
        third_kernel,
        (shape((32 * 10, BLOCK), BF16),),
        [VMEM],
        (s2,),
        [pltpu.VMEM((peers * wide + ROOM, BLOCK), F32)],
        flops=10_000_000,
    )
    s3 = lax.all_to_all(
        s3.reshape(32 * 5, 2, BLOCK), both, split_axis=0, concat_axis=0, tiled=True,
        axis_index_groups=device_groups(("z", "y")),
    ).reshape(32 * 10, BLOCK)
    (grad_feats,) = call(
        feats_kernel,
        (shape((nodes, width), BF16),),
        [VMEM] * 5,
        (s2, recv, base, coords, proj.T),
        flops=150_000_000,
    )
    (s4,) = call(
        fourth_kernel,
        (shape((8, 160, BLOCK), BF16),),
        [VMEM],
        (s3,),
        [pltpu.VMEM((32 * 10 + 2 * ROOM, BLOCK), F32)],
    )
    s4 = lax.all_to_all(
        s4, both, split_axis=0, concat_axis=0, tiled=True,
        axis_index_groups=device_groups(("x", "core")),
    )
    grad_self, grad_neigh, grad_lift, grad_proj = call(
        lambda *refs: last_kernel(norm_scale, *refs),
        (
            shape((width, width), F32),
            shape((width, width), F32),
            shape((rank, width), F32),
            shape((rank, width), F32),
        ),
        [VMEM],
        (s4,),
        [pltpu.VMEM((4, width + ROOM, BLOCK), F32), pltpu.VMEM((4, rank + ROOM, BLOCK), F32)],
    )
    return (grad_feats, grad_self, grad_neigh, grad_lift, grad_proj.T)


def solution(mesh):
    both = ("hst", "dev")
    row, cube = P(both, None), P(both, None, None)
    placed = (
        (row,) * 5 + (P(),) * 4 + (cube,) + (row,) * 7 + (cube,) + (row,) + (cube,)
    )
    return jax.shard_map(
        body,
        mesh=mesh,
        in_specs=placed,
        out_specs=(row, P(), P(), P(), P()),
        check_vma=False,
    )
```
